32 devices in a mesh: leaf: 32 (over z, y, x, core).
Axes of the slice: x: 2, y: 2, z: 4, core: 2. Of those that a mesh axis runs over, the one named last changes fastest.
Arguments:
- points: float32 [16, 65536], P(None, 'leaf'), may hold values from -6 to 6
- charges: float32 [16, 65536], P(None, 'leaf'), may hold values from -0.6 to 0.6
- near_list: int32 [128, 32], P('leaf'), may hold values from 0 to 127, as said below
- near_count: int32 [128], P('leaf'), may hold values from 1 to 32, as said below
- leaf_basis: float32 [65536, 256], P('leaf'), may hold values from -0.75 to 0.75
- device_basis: float32 [32768, 256], P('leaf'), may hold values from -0.1875 to 0.1875
- device_skeleton: int32 [32, 256], P('leaf'), may hold values from 0 to 2047, as said below
- group_basis: float32 [1024, 2048], P(None, 'leaf'), may hold values from -0.1875 to 0.1875
- group_skeleton: int32 [2048], P('leaf'), may hold values from 0 to 1023, as said below
- cluster_basis: float32 [1024, 512], P(None, 'leaf'), may hold values from -0.1875 to 0.1875
- cluster_skeleton: int32 [512], P('leaf'), may hold values from 0 to 1023, as said below
Outputs:
- potentials: float32 [16, 65536], P(None, 'leaf')
The draws below stay inside these ranges and needn't reach their ends.
Inputs may be any that keep to these rules, and one draw needn't show every extreme that they name: `near_list`: row l names leaves whose devices lie at most 8 devices from leaf l's device; its first entry is l, its first near_count[l] entries are distinct, and the later entries repeat l. Only the first near_count[l] entries of leaf l's list count. `device_skeleton`: each row holds distinct indices into its device's points. `group_skeleton`: entries g * 256 to (g + 1) * 256 - 1 are distinct indices into the 1024 skeleton points of group g's four devices, side by side in device order. `cluster_skeleton`: entries c * 256 to (c + 1) * 256 - 1 are distinct indices into the 1024 skeleton points of cluster c's four groups, side by side in group order.
All inputs are finite; a program needn't handle non-finite values.
Results may differ from the reference program's by a relative error of at most 0.0034.
Values sent between devices are 32-bit elements; how exact they have to be, the bound alone decides.
A program may use at most 64 MiB of HBM per device.

```python
import jax
import jax.numpy as jnp
from jax import lax

F = 16
R = 16
LEAF = 512
S = 256
NBR = 32
REACH = 8
LEAVES_DEV = 4
NLEAVES = 128
NPTS = 65536
N_LEAF = 32


def near_tables(key):
    base_key = jax.random.fold_in(key, 17)
    device_total = NLEAVES // LEAVES_DEV
    span = (2 * REACH + 1) * LEAVES_DEV
    leaves = jnp.arange(NLEAVES, dtype=jnp.int32)
    owners = leaves // LEAVES_DEV
    offsets = jnp.arange(span, dtype=jnp.int32)
    candidates = (owners[:, None] - REACH) * LEAVES_DEV + offsets[None, :]
    usable = (candidates >= 0) & (candidates < NLEAVES) & (candidates != leaves[:, None])
    noise = jax.random.randint(jax.random.fold_in(base_key, 1), (NLEAVES, span), 0, 1 << 18)
    scores = jnp.where(usable, noise * 1024 + offsets[None, :], (1 << 29) + offsets[None, :])
    order = jnp.argsort(scores, axis=1)
    chosen = jnp.take_along_axis(candidates, order[:, :NBR - 1], axis=1)
    usable_count = jnp.sum(usable.astype(jnp.int32), axis=1)
    device_load = jax.random.randint(jax.random.fold_in(base_key, 2), (device_total,), 1, 5)
    drawn = jax.random.randint(jax.random.fold_in(base_key, 3), (NLEAVES,), 0, 1 << 20)
    ceiling = 8 * device_load[owners]
    counts = 1 + drawn % ceiling
    fullest = jax.random.randint(jax.random.fold_in(base_key, 4), (), REACH * LEAVES_DEV, NLEAVES - REACH * LEAVES_DEV)
    emptiest = jax.random.randint(jax.random.fold_in(base_key, 5), (), 0, REACH * LEAVES_DEV)
    counts = jnp.where(leaves == fullest, NBR, counts)
    counts = jnp.where(leaves == emptiest, 1, counts)
    counts = jnp.minimum(counts, 1 + usable_count)
    lists = jnp.concatenate([leaves[:, None], chosen], axis=1)
    slots = jnp.arange(NBR, dtype=jnp.int32)
    lists = jnp.where(slots[None, :] < counts[:, None], lists, leaves[:, None])
    return (lists.astype(jnp.int32), counts.astype(jnp.int32))


def draw_near_list(key, part):
    return near_tables(key)[0]


def draw_near_count(key, part):
    return near_tables(key)[1]


def node_skeleton(key, nodes, pool, picks):
    node_keys = jax.random.split(key, nodes)
    orders = jax.vmap(lambda one_key: jax.random.permutation(one_key, pool))(node_keys)
    marked = jax.random.randint(jax.random.fold_in(key, 7), (), 0, nodes)
    chosen_row = orders[marked]
    spot_high = jnp.argmax(chosen_row == pool - 1)
    chosen_row = chosen_row.at[spot_high].set(chosen_row[0]).at[0].set(pool - 1)
    spot_low = jnp.argmax(chosen_row == 0)
    chosen_row = chosen_row.at[spot_low].set(chosen_row[1]).at[1].set(0)
    orders = orders.at[marked].set(chosen_row)
    return orders[:, :picks].astype(jnp.int32)


def draw_device_skeleton(key, part):
    return node_skeleton(jax.random.fold_in(key, 31), NLEAVES // LEAVES_DEV, LEAVES_DEV * LEAF, S)


def draw_group_skeleton(key, part):
    return node_skeleton(jax.random.fold_in(key, 37), NLEAVES // LEAVES_DEV // 4, 4 * S, S).reshape(-1)


def draw_cluster_skeleton(key, part):
    return node_skeleton(jax.random.fold_in(key, 41), NLEAVES // LEAVES_DEV // 16, 4 * S, S).reshape(-1)


def block_levels(key, dims, pieces, low, top_value):
    gain, own = 1.0, jax.random.fold_in(key, 6)
    for position, parts in pieces:
        steps = jnp.exp(jax.random.uniform(jax.random.fold_in(own, position), (parts,), jnp.float32, low / len(pieces), top_value / len(pieces)))
        gain = gain * jnp.repeat(steps, dims[position] // parts).reshape([-1 if axis == position else 1 for axis in range(len(dims))])
    return gain


def centred(rng, dims, width, most, cuts=(), kind=jnp.bfloat16):
    loudness = block_levels(rng, dims, cuts, -0.22, 0.18) if cuts else 1.0
    values = jax.random.normal(rng, dims, jnp.float32) * width * loudness
    return jnp.minimum(jnp.maximum(values, -most), most).astype(kind)


def setup_inputs(seed: int = 0) -> dict:
    streams_of = jax.random.split(jax.random.key(seed), 12)
    points = centred(streams_of[0], (F, NPTS), 1.0, 6.0, ((1, 32),), jnp.float32)
    charges = centred(streams_of[1], (R, NPTS), 0.1, 0.6, ((1, 32),), jnp.float32)
    near_list = draw_near_list(jax.random.fold_in(streams_of[11], 71), 0)
    near_count = draw_near_count(jax.random.fold_in(streams_of[11], 71), 0)
    leaf_basis = centred(streams_of[4], (NPTS, S), (S // 4) ** -0.5, 0.75, ((0, 32),), jnp.float32)
    device_basis = centred(streams_of[5], (NLEAVES * S, S), (LEAVES_DEV * S) ** -0.5, 0.1875, ((0, 32),), jnp.float32)
    device_skeleton = draw_device_skeleton(jax.random.fold_in(streams_of[11], 71), 0)
    group_basis = centred(streams_of[7], (4 * S, N_LEAF * S // 4), (4 * S) ** -0.5, 0.1875, ((1, 32),), jnp.float32)
    group_skeleton = draw_group_skeleton(jax.random.fold_in(streams_of[11], 71), 0)
    cluster_basis = centred(streams_of[9], (4 * S, N_LEAF * S // 16), (4 * S) ** -0.5, 0.1875, ((1, 32),), jnp.float32)
    cluster_skeleton = draw_cluster_skeleton(jax.random.fold_in(streams_of[11], 71), 0)
    return {"points": points, "charges": charges, "near_list": near_list, "near_count": near_count, "leaf_basis": leaf_basis, "device_basis": device_basis, "device_skeleton": device_skeleton, "group_basis": group_basis, "group_skeleton": group_skeleton, "cluster_basis": cluster_basis, "cluster_skeleton": cluster_skeleton}


inverse_spread = 1.0 / 16.0
exact_mode = lax.Precision.HIGHEST


def kernel_of(left_points, right_points):
    cross_terms = jnp.dot(left_points.T, right_points, precision=exact_mode, preferred_element_type=jnp.float32)
    left_square = jnp.sum(left_points * left_points, axis=0)
    right_square = jnp.sum(right_points * right_points, axis=0)
    return jnp.exp(-(left_square[:, None] + right_square[None, :] - 2.0 * cross_terms) * inverse_spread)


def near_field(points, charges, near_list, near_count):
    def per_leaf(leaf_index):
        start = (leaf_index * LEAF).astype(jnp.int32)
        target = lax.dynamic_slice_in_dim(points, start, LEAF, 1)

        def add_tile(slot_index, running):
            other = (near_list[leaf_index, slot_index] * LEAF).astype(jnp.int32)
            source = lax.dynamic_slice_in_dim(points, other, LEAF, 1)
            source_charges = lax.dynamic_slice_in_dim(charges, other, LEAF, 1).astype(jnp.bfloat16)
            kernel_tile = kernel_of(target, source).astype(jnp.bfloat16)
            return running + lax.dot_general(source_charges, kernel_tile, (((1,), (1,)), ((), ())), preferred_element_type=jnp.float32)

        return lax.fori_loop(0, near_count[leaf_index], add_tile, jnp.zeros((R, LEAF), jnp.float32))

    blocks = lax.map(per_leaf, jnp.arange(NLEAVES, dtype=jnp.int32))
    return jnp.transpose(blocks, (1, 0, 2)).reshape(R, NLEAVES * LEAF)


def pick_columns(values, indices):
    full_index = jnp.broadcast_to(indices[None], (values.shape[0],) + indices.shape)
    return jnp.take_along_axis(values, full_index, axis=2)


def reference(points, charges, near_list, near_count, leaf_basis, device_basis, device_skeleton, group_basis, group_skeleton, cluster_basis, cluster_skeleton):
    near = near_field(points, charges, near_list, near_count)
    device_total = NLEAVES // LEAVES_DEV
    group_total = device_total // 4
    cluster_total = device_total // 16
    points_each = LEAVES_DEV * LEAF
    leaf_blocks = leaf_basis.reshape(NLEAVES, LEAF, S)
    leaf_weights = jnp.einsum('lps,rlp->rls', leaf_blocks, charges.reshape(R, NLEAVES, LEAF), precision=exact_mode)
    device_blocks = device_basis.reshape(device_total, LEAVES_DEV * S, S)
    device_weights = jnp.einsum('dks,rdk->rds', device_blocks, leaf_weights.reshape(R, device_total, LEAVES_DEV * S), precision=exact_mode)
    device_points = pick_columns(points.reshape(F, device_total, points_each), device_skeleton)
    group_blocks = group_basis.reshape(4 * S, group_total, S)
    group_weights = jnp.einsum('kgs,rgk->rgs', group_blocks, device_weights.reshape(R, group_total, 4 * S), precision=exact_mode)
    group_points = pick_columns(device_points.reshape(F, group_total, 4 * S), group_skeleton.reshape(group_total, S))
    cluster_blocks = cluster_basis.reshape(4 * S, cluster_total, S)
    cluster_weights = jnp.einsum('kgs,rgk->rgs', cluster_blocks, group_weights.reshape(R, cluster_total, 4 * S), precision=exact_mode)
    cluster_points = pick_columns(group_points.reshape(F, cluster_total, 4 * S), cluster_skeleton.reshape(cluster_total, S))
    flat_points = cluster_points.reshape(F, cluster_total * S)
    flat_weights = cluster_weights.reshape(R, cluster_total * S)
    cluster_of = jnp.arange(cluster_total * S) // S
    top_kernel = kernel_of(flat_points, flat_points) * (cluster_of[:, None] != cluster_of[None, :])
    top = jnp.dot(flat_weights, top_kernel.T, precision=exact_mode)
    child_of = jnp.arange(4 * S) // S
    sibling_mask = child_of[:, None] != child_of[None, :]

    def side_of(pair):
        block_points, block_weights = pair
        return jnp.dot(block_weights, (kernel_of(block_points, block_points) * sibling_mask).T, precision=exact_mode)

    side_parts = lax.map(side_of, (jnp.moveaxis(group_points.reshape(F, cluster_total, 4 * S), 1, 0), jnp.moveaxis(group_weights.reshape(R, cluster_total, 4 * S), 1, 0)))
    side = jnp.moveaxis(side_parts, 0, 1).reshape(R, group_total, S)
    from_top = jnp.einsum('kgs,rgs->rgk', cluster_blocks, top.reshape(R, cluster_total, S), precision=exact_mode)
    down_group = side + from_top.reshape(R, group_total, S)
    down_device = jnp.einsum('kgs,rgs->rgk', group_blocks, down_group, precision=exact_mode).reshape(R, device_total, S)
    down_leaf = jnp.einsum('dks,rds->rdk', device_blocks, down_device, precision=exact_mode).reshape(R, NLEAVES, S)
    far_field = jnp.einsum('lps,rls->rlp', leaf_blocks, down_leaf, precision=exact_mode).reshape(R, NPTS)
    return near + far_field
```

```python
import math

import jax
import jax.numpy as jnp
from jax import lax
from jax.experimental import pallas as pl
from jax.experimental.pallas import tpu as pltpu
from jax.sharding import PartitionSpec as P

F = 16
R = 16
LEAF = 512
S = 256
REACH = 8
LEAVES_DEV = 4


inverse_spread = 1.0 / 16.0
exact_mode = lax.Precision.HIGHEST


def passed_along(value, axis, steps):
    count = lax.axis_size(axis)
    leading, last = (max(0, -steps), min(count, count - steps))
    return lax.ppermute(value, axis, [(source, source + steps) for source in range(leading, last)])


def partner_2(value, axis, stride):
    mask = 2**stride
    pairs = [(source, source ^ mask) for source in range(lax.axis_size(axis))]
    return lax.ppermute(value, axis, pairs)


def kernel_of(left_points, right_points):
    cross_terms = jnp.dot(
        left_points.T, right_points, precision=exact_mode, preferred_element_type=jnp.float32
    )
    left_square = jnp.sum(left_points * left_points, axis=0)
    right_square = jnp.sum(right_points * right_points, axis=0)
    return jnp.exp(
        -(left_square[:, None] + right_square[None, :] - 2.0 * cross_terms) * inverse_spread
    )


def near_window(payload):
    pieces = []
    for offset in range(-REACH, REACH + 1):
        if offset == 0:
            pieces.append(payload)
        else:
            pieces.append(passed_along(payload, "leaf", -offset))
    return jnp.stack(pieces, axis=0)


def split3(value):
    high = value.astype(jnp.bfloat16)
    rest = value - high.astype(jnp.float32)
    middle = rest.astype(jnp.bfloat16)
    low = (rest - middle.astype(jnp.float32)).astype(jnp.bfloat16)
    return high, middle, low


def norm_rows(squares, first):
    high, middle, low = (piece.astype(jnp.float32) for piece in split3(squares))
    row = lax.broadcasted_iota(jnp.int32, (16, squares.shape[1]), 0)
    ones = 3 - first
    block = jnp.where((row >= ones) & (row < ones + 3), 1.0, 0.0)
    block = jnp.where(row == first, high, block)
    block = jnp.where(row == first + 1, middle, block)
    return jnp.where(row == first + 2, low, block)


def near_kernel(list_ref, count_ref, points_ref, window_ref, far_ref, out_ref, source, charge, target):
    leaf = source.shape[2]
    leaves_dev = points_ref.shape[1] // leaf
    scale = inverse_spread * math.log2(math.e)

    def prepare(device, carry):
        for inner in range(leaves_dev):
            columns = slice(inner * leaf, (inner + 1) * leaf)
            block = window_ref[device, 0:F, columns]
            slot = device * leaves_dev + inner
            high, middle, low = split3(block)
            squares = jnp.sum(block * block, axis=0, keepdims=True) * (-scale)
            norms = norm_rows(squares, 3).astype(jnp.bfloat16)
            pieces = (high, middle, high, low, high, middle, norms, jnp.zeros_like(norms))
            for place, piece in enumerate(pieces):
                source[slot, place * 16 : (place + 1) * 16, :] = piece
            charge[slot] = window_ref[device, F : F + R, columns].astype(jnp.bfloat16)
        return carry

    lax.fori_loop(0, window_ref.shape[0], prepare, 0)

    for inner in range(leaves_dev):
        columns = slice(inner * leaf, (inner + 1) * leaf)
        block = points_ref[:, columns]
        high, middle, low = (p.astype(jnp.float32) for p in split3(block * (2.0 * scale)))
        squares = jnp.sum(block * block, axis=0, keepdims=True) * (-scale)
        norms = norm_rows(squares, 0)
        stacked = jnp.concatenate(
            [high, high, middle, high, low, middle, norms, jnp.zeros_like(norms)], axis=0
        )
        target[...] = stacked.T.astype(jnp.bfloat16)
        count = count_ref[inner]

        def two_tiles(step, running):
            for side in range(2):
                slot = step * 2 + side
                picked = list_ref[inner, slot]
                live = (slot < count).astype(jnp.float32)
                power = jnp.dot(target[...], source[picked], preferred_element_type=jnp.float32)
                tile = jnp.exp2(power).astype(jnp.bfloat16)
                weights = (charge[picked].astype(jnp.float32) * live).astype(jnp.bfloat16)
                running = running + lax.dot_general(
                    weights, tile, (((1,), (1,)), ((), ())), preferred_element_type=jnp.float32
                )
            return running

        total = lax.fori_loop(0, (count + 1) // 2, two_tiles, jnp.zeros((R, leaf), jnp.float32))
        out_ref[:, columns] = total + far_ref[:, columns]


def near_field(points, window, near_list, near_count, far):
    devices, _, width = window.shape
    leaves_dev = near_list.shape[0]
    leaf = width // leaves_dev
    first_leaf = (lax.axis_index("leaf") - REACH) * leaves_dev
    slots = devices * leaves_dev
    vmem = pl.BlockSpec(memory_space=pltpu.VMEM)
    smem = pl.BlockSpec(memory_space=pltpu.SMEM)
    return pl.pallas_call(
        near_kernel,
        out_shape=jax.ShapeDtypeStruct((R, width), jnp.float32),
        in_specs=[smem, smem, vmem, vmem, vmem],
        out_specs=vmem,
        scratch_shapes=[
            pltpu.VMEM((slots, 128, leaf), jnp.bfloat16),
            pltpu.VMEM((slots, R, leaf), jnp.bfloat16),
            pltpu.VMEM((leaf, 128), jnp.bfloat16),
        ],
        compiler_params=pltpu.CompilerParams(vmem_limit_bytes=48 * 1024 * 1024),
        name="near_tiles",
    )(near_list - first_leaf, near_count, points, window, far)


def collect_pairwise(payload, bit_list):
    position = lax.axis_index("leaf")
    for bit in bit_list:
        partner = partner_2(payload, "leaf", bit)
        upper_half = position >> bit & 1 == 1
        payload = jnp.where(
            upper_half,
            jnp.concatenate([partner, payload], 1),
            jnp.concatenate([payload, partner], 1),
        )
    return payload


def spread_pairwise(partial_sum, bit_list):
    position = lax.axis_index("leaf")
    for bit in bit_list:
        half = partial_sum.shape[1] // 2
        lower_columns = partial_sum[:, :half]
        upper_columns = partial_sum[:, half:]
        upper_half = position >> bit & 1 == 1
        outgoing = jnp.where(upper_half, lower_columns, upper_columns)
        incoming = partner_2(outgoing, "leaf", bit)
        partial_sum = jnp.where(upper_half, upper_columns, lower_columns) + incoming
    return partial_sum


def right_product(left_matrix, right_matrix):
    return lax.dot_general(
        left_matrix,
        right_matrix,
        (((1,), (1,)), ((), ())),
        precision=exact_mode,
        preferred_element_type=jnp.float32,
    )


def shards(
    points,
    charges,
    near_list,
    near_count,
    leaf_basis,
    device_basis,
    device_skeleton,
    group_basis,
    group_skeleton,
    cluster_basis,
    cluster_skeleton,
):
    payload = jnp.concatenate([points, charges], axis=0)
    window = near_window(payload)
    position = lax.axis_index("leaf")
    leaf_blocks = leaf_basis.reshape(LEAVES_DEV, LEAF, S)
    leaf_weights = jnp.einsum(
        "lps,rlp->rls", leaf_blocks, charges.reshape(R, LEAVES_DEV, LEAF), precision=exact_mode
    )
    device_weights = jnp.dot(
        leaf_weights.reshape(R, LEAVES_DEV * S), device_basis, precision=exact_mode
    )
    device_points = jnp.take(points, device_skeleton[0], axis=1)
    device_payload = jnp.concatenate([device_points, device_weights], axis=0)
    group_stack = collect_pairwise(device_payload, (0, 1))
    quarter_weights = jnp.dot(group_stack[F:], group_basis, precision=exact_mode)
    quarter_points = jnp.take(group_stack[:F], group_skeleton, axis=1)
    quarter_payload = jnp.concatenate([quarter_points, quarter_weights], axis=0)
    cluster_stack = collect_pairwise(quarter_payload, (0, 1, 2, 3))
    cluster_points = cluster_stack[:F]
    cluster_weights = cluster_stack[F:]
    part_weights = jnp.dot(cluster_weights, cluster_basis, precision=exact_mode)
    part_points = jnp.take(cluster_points, cluster_skeleton, axis=1)
    all_nodes = lax.all_gather(
        jnp.concatenate([part_points, part_weights], axis=0), "leaf", axis=1, tiled=True
    )
    cluster_of = jnp.arange(all_nodes.shape[1]) // S
    top_kernel = kernel_of(part_points, all_nodes[:F]) * (cluster_of != position // 16)[None, :]
    top_part = right_product(all_nodes[F:], top_kernel)
    group_of = jnp.arange(4 * S) // S
    side_kernel = (
        kernel_of(quarter_points, cluster_points) * (group_of != position % 16 // 4)[None, :]
    )
    side_part = right_product(cluster_weights, side_kernel)
    from_top = right_product(top_part, cluster_basis)
    down_group = side_part + spread_pairwise(from_top, (3, 2, 1, 0))
    from_group = right_product(down_group, group_basis)
    down_device = spread_pairwise(from_group, (1, 0))
    down_leaves = right_product(down_device, device_basis)
    far_field = jnp.einsum(
        "lps,rls->rlp", leaf_blocks, down_leaves.reshape(R, LEAVES_DEV, S), precision=exact_mode
    )
    far_field = far_field.reshape(R, LEAVES_DEV * LEAF)
    return near_field(points, window, near_list, near_count, far_field)


def solution(mesh):
    return jax.shard_map(
        shards,
        mesh=mesh,
        in_specs=(
            P(None, "leaf"),
            P(None, "leaf"),
            P("leaf", None),
            P("leaf"),
            P("leaf", None),
            P("leaf", None),
            P("leaf", None),
            P(None, "leaf"),
            P("leaf"),
            P(None, "leaf"),
            P("leaf"),
        ),
        out_specs=P(None, "leaf"),
        check_vma=False,
    )
```

```python
import functools
import math

import jax
import jax.numpy as jnp
from jax import lax
from jax.experimental import pallas as pl
from jax.experimental.pallas import tpu as pltpu
from jax.sharding import PartitionSpec as P

F = 16
R = 16
S = 256
REACH = 8
LEAVES_DEV = 4


inverse_spread = 1.0 / 16.0


def split3(value):
    high = value.astype(jnp.bfloat16)
    rest = value - high.astype(jnp.float32)
    middle = rest.astype(jnp.bfloat16)
    low = (rest - middle.astype(jnp.float32)).astype(jnp.bfloat16)
    return high, middle, low


def norm_rows(squares, first):
    high, middle, low = (piece.astype(jnp.float32) for piece in split3(squares))
    row = lax.broadcasted_iota(jnp.int32, (16, squares.shape[1]), 0)
    ones = 3 - first
    block = jnp.where((row >= ones) & (row < ones + 3), 1.0, 0.0)
    block = jnp.where(row == first, high, block)
    block = jnp.where(row == first + 1, middle, block)
    return jnp.where(row == first + 2, low, block)


def split2(value):
    high = value.astype(jnp.bfloat16)
    return high, (value - high.astype(jnp.float32)).astype(jnp.bfloat16)


def product(left, right, contract):
    dims = (((1,), (contract,)), ((), ()))
    left_high, left_low = split2(left)
    right_high, right_low = split2(right)
    rows = left.shape[0]
    both = lax.dot_general(
        jnp.concatenate([left_high, left_low], axis=0),
        right_high,
        dims,
        preferred_element_type=jnp.float32,
    )
    rest = lax.dot_general(left_high, right_low, dims, preferred_element_type=jnp.float32)
    return both[:rows] + (both[rows:] + rest)


def pick(values, one_hot):
    stacked = jnp.concatenate(list(split3(values)), axis=0)
    picked = jnp.dot(stacked, one_hot, preferred_element_type=jnp.float32)
    rows = values.shape[0]
    return picked[:rows] + picked[rows : 2 * rows] + picked[2 * rows :]


def source_rows(block):
    scale = inverse_spread * math.log2(math.e)
    high, middle, low = split3(block)
    squares = jnp.sum(block * block, axis=0, keepdims=True) * (-scale)
    norms = norm_rows(squares, 3).astype(jnp.bfloat16)
    return (high, middle, high, low, high, middle, norms, jnp.zeros_like(norms))


def target_rows(block):
    scale = inverse_spread * math.log2(math.e)
    high, middle, low = (p.astype(jnp.float32) for p in split3(block * (2.0 * scale)))
    squares = jnp.sum(block * block, axis=0, keepdims=True) * (-scale)
    norms = norm_rows(squares, 0)
    stacked = jnp.concatenate(
        [high, high, middle, high, low, middle, norms, jnp.zeros_like(norms)], axis=0
    )
    return stacked.T.astype(jnp.bfloat16)


def far_sum(weights, targets, sources):
    power = jnp.dot(
        target_rows(targets),
        jnp.concatenate(list(source_rows(sources)), axis=0),
        preferred_element_type=jnp.float32,
    )
    return product(weights, jnp.exp2(power), 1)


def one_hot_of(indices, rows, first):
    row = lax.broadcasted_iota(jnp.int32, (rows, indices.shape[1]), 0) + first
    return (row == indices).astype(jnp.float32).astype(jnp.bfloat16)


def near_kernel(list_ref, count_ref, points_ref, window_ref, far_ref, out_ref, source, charge, target):
    leaf = source.shape[2]
    leaves_dev = points_ref.shape[1] // leaf

    def prepare(device, carry):
        for inner in range(leaves_dev):
            columns = slice(inner * leaf, (inner + 1) * leaf)
            block = window_ref[device, 0:F, columns]
            slot = device * leaves_dev + inner
            pieces = source_rows(block)
            for place, piece in enumerate(pieces):
                source[slot, place * 16 : (place + 1) * 16, :] = piece
            charge[slot] = window_ref[device, F : F + R, columns].astype(jnp.bfloat16)
        return carry

    lax.fori_loop(0, window_ref.shape[0], prepare, 0)

    for inner in range(leaves_dev):
        columns = slice(inner * leaf, (inner + 1) * leaf)
        block = points_ref[:, columns]
        target[...] = target_rows(block)
        count = count_ref[inner]

        def two_tiles(step, running):
            for side in range(2):
                slot = step * 2 + side
                picked = list_ref[inner, slot]
                live = (slot < count).astype(jnp.float32)
                power = jnp.dot(target[...], source[picked], preferred_element_type=jnp.float32)
                tile = jnp.exp2(power).astype(jnp.bfloat16)
                weights = (charge[picked].astype(jnp.float32) * live).astype(jnp.bfloat16)
                running = running + lax.dot_general(
                    weights, tile, (((1,), (1,)), ((), ())), preferred_element_type=jnp.float32
                )
            return running

        total = lax.fori_loop(0, (count + 1) // 2, two_tiles, jnp.zeros((R, leaf), jnp.float32))
        out_ref[:, columns] = total + far_ref[:, columns]


def near_field(points, window, near_list, near_count, far):
    devices, _, width = window.shape
    leaves_dev = near_list.shape[0]
    leaf = width // leaves_dev
    first_leaf = (lax.axis_index("leaf") - REACH) * leaves_dev
    slots = devices * leaves_dev
    vmem = pl.BlockSpec(memory_space=pltpu.VMEM)
    smem = pl.BlockSpec(memory_space=pltpu.SMEM)
    return pl.pallas_call(
        near_kernel,
        out_shape=jax.ShapeDtypeStruct((R, width), jnp.float32),
        in_specs=[smem, smem, vmem, vmem, vmem],
        out_specs=vmem,
        scratch_shapes=[
            pltpu.VMEM((slots, 128, leaf), jnp.bfloat16),
            pltpu.VMEM((slots, R, leaf), jnp.bfloat16),
            pltpu.VMEM((leaf, 128), jnp.bfloat16),
        ],
        compiler_params=pltpu.CompilerParams(vmem_limit_bytes=48 * 1024 * 1024),
        name="near_tiles",
    )(near_list - first_leaf, near_count, points, window, far)


def tree_kernel(
    n,
    points,
    charges,
    leaf_basis,
    device_basis,
    device_skeleton,
    group_basis,
    group_skeleton,
    cluster_basis,
    cluster_skeleton,
    window,
    far,
    group_own,
    cluster_own,
    group_rows,
    cluster_rows,
    device_nodes,
    quarters,
    stack,
    parts,
    parts_turned,
    local_sem,
    window_send,
    forward_send,
    window_recv,
    rows_send,
    rows_recv,
    cluster_rows_send,
    cluster_rows_recv,
    device_send,
    device_recv,
    quarter_send,
    quarter_recv,
    part_send,
    part_recv,
):
    me = lax.axis_index("leaf")
    group = device_nodes.shape[0]
    cluster = quarters.shape[0]
    quarter = group_basis.shape[1]
    part = cluster_basis.shape[1]
    leaf = points.shape[1] // LEAVES_DEV
    place, child = me % cluster, me % group
    group_first, cluster_first = me - child, me - place
    group_in_cluster = place // group
    core = me % 2
    sibling = me + 1 - 2 * core
    middle_slot = REACH

    def send(source, destination, send_sem, recv_sem, device):
        return pltpu.make_async_remote_copy(
            src_ref=source,
            dst_ref=destination,
            send_sem=send_sem,
            recv_sem=recv_sem,
            device_id=(device,),
            device_id_type=pl.DeviceIdType.MESH,
        )

    def each(count, body):
        def step(index, carry):
            body(index)
            return carry

        lax.fori_loop(0, count, step, 0)

    def columns_of(index):
        return pl.ds(pl.multiple_of(index * S, S), S)

    barrier = pltpu.get_barrier_semaphore()

    def greet(index):
        other = (me + 1 + index) % n
        pl.semaphore_signal(
            barrier, inc=1, device_id=(other,), device_id_type=pl.DeviceIdType.MESH
        )

    each(n - 1, greet)
    own_points = pltpu.make_async_copy(
        points, window.at[middle_slot, pl.ds(0, F)], local_sem.at[0]
    )
    own_charges = pltpu.make_async_copy(
        charges, window.at[middle_slot, pl.ds(F, R)], local_sem.at[1]
    )
    own_points.start()
    own_charges.start()
    group_own[...] = group_basis[...].T
    cluster_own[...] = cluster_basis[...].T
    own_points.wait()
    own_charges.wait()
    pl.semaphore_wait(barrier, n - 1)

    def lane_offset(index):
        return jnp.where(index < REACH // 2, index - REACH // 2, index - REACH // 2 + 1) * 2

    def lane_copy(index):
        offset = lane_offset(index)
        slot = middle_slot - offset
        return send(
            window.at[middle_slot],
            window.at[slot],
            window_send.at[index],
            window_recv.at[slot],
            jnp.clip(me + offset, 0, n - 1),
        )

    def inside(device):
        return (device >= 0) & (device < n)

    def start_lane(index):
        @pl.when(inside(me + lane_offset(index)))
        def _():
            lane_copy(index).start()

    def forward_copy(index):
        slot = index * 2
        landing = jnp.clip(slot - 1 + 2 * core, 0, 2 * REACH)
        return send(
            window.at[slot],
            window.at[landing],
            forward_send.at[index],
            window_recv.at[landing],
            sibling,
        )

    def forwarded(index):
        slot = index * 2
        landing = slot - 1 + 2 * core
        return inside(me + slot - middle_slot) & (landing >= 0) & (landing <= 2 * REACH)

    def arrived(slot):
        send(
            window.at[slot], window.at[slot], window_send.at[0], window_recv.at[slot], sibling
        ).wait_recv()

    each(REACH, start_lane)
    forward_copy(REACH // 2).start()

    def group_rows_copy(index):
        other = (child + 1 + index) % group
        return send(
            group_own.at[:, columns_of(other)],
            group_rows.at[child],
            rows_send.at[index],
            rows_recv.at[child],
            group_first + other,
        )

    def cluster_rows_copy(index):
        other = (place + 1 + index) % cluster
        return send(
            cluster_own.at[:, columns_of(other // group)],
            cluster_rows.at[place],
            cluster_rows_send.at[index],
            cluster_rows_recv.at[place],
            cluster_first + other,
        )

    each(group - 1, lambda index: group_rows_copy(index).start())
    each(cluster - 1, lambda index: cluster_rows_copy(index).start())
    group_rows[child] = group_own[:, columns_of(child)]
    cluster_rows[place] = cluster_own[:, columns_of(group_in_cluster)]

    device_weights = jnp.zeros((R, S), jnp.float32)
    device_points = jnp.zeros((F, S), jnp.float32)
    for inner in range(LEAVES_DEV):
        rows = slice(inner * leaf, (inner + 1) * leaf)
        leaf_weights = product(charges[:, rows], leaf_basis[rows, :], 0)
        device_weights += product(
            leaf_weights, device_basis[inner * S : (inner + 1) * S, :], 0
        )
        device_points += pick(
            points[:, rows], one_hot_of(device_skeleton[...], leaf, inner * leaf)
        )
    device_nodes[child, 0:F, :] = device_points
    device_nodes[child, F : F + R, :] = device_weights

    def device_copy(index):
        other = (child + 1 + index) % group
        return send(
            device_nodes.at[child],
            device_nodes.at[child],
            device_send.at[index],
            device_recv.at[child],
            group_first + other,
        )

    def device_arrived(index):
        other = (child + 1 + index) % group
        send(
            device_nodes.at[other],
            device_nodes.at[other],
            device_send.at[index],
            device_recv.at[other],
            group_first + other,
        ).wait_recv()

    each(group - 1, lambda index: device_copy(index).start())
    each(group - 1, device_arrived)

    quarter_weights = jnp.zeros((R, quarter), jnp.float32)
    quarter_points = jnp.zeros((F, quarter), jnp.float32)
    for inner in range(group):
        quarter_weights += product(
            device_nodes[inner, F : F + R, :], group_basis[inner * S : (inner + 1) * S, :], 0
        )
        quarter_points += pick(
            device_nodes[inner, 0:F, :], one_hot_of(group_skeleton[...], S, inner * S)
        )
    quarters[place] = jnp.concatenate([quarter_points, quarter_weights], axis=1)

    def quarter_copy(index):
        other = (place + 1 + index) % cluster
        return send(
            quarters.at[place],
            quarters.at[place],
            quarter_send.at[index],
            quarter_recv.at[place],
            cluster_first + other,
        )

    def quarter_arrived(index):
        other = (place + 1 + index) % cluster
        send(
            quarters.at[other],
            quarters.at[other],
            quarter_send.at[index],
            quarter_recv.at[other],
            cluster_first + other,
        ).wait_recv()

    each(cluster - 1, lambda index: quarter_copy(index).start())
    each(cluster - 1, quarter_arrived)

    lane = lax.broadcasted_iota(jnp.int32, (F, 2 * quarter), 1)
    for pair in range(cluster // 2):
        even, odd = quarters[2 * pair], quarters[2 * pair + 1]
        columns = slice(pair * 2 * quarter, (pair + 1) * 2 * quarter)
        stack[0:F, columns] = jnp.where(lane < quarter, even, pltpu.roll(odd, quarter, 1))
        stack[F : F + R, columns] = jnp.where(lane < quarter, pltpu.roll(even, quarter, 1), odd)

    whole = stack[...]
    column = lax.broadcasted_iota(jnp.int32, (part, whole.shape[1]), 1)
    one_hot = (column == cluster_skeleton[...]).astype(jnp.float32).astype(jnp.bfloat16)
    turned = (((1,), (1,)), ((), ()))
    high, middle, low = (
        lax.dot_general(one_hot, piece, turned, preferred_element_type=jnp.float32)
        for piece in split3(whole)
    )
    part_points = high + middle + low
    part_weights = product(cluster_own[...], whole, 1)
    kind = lax.broadcasted_iota(jnp.int32, part_points.shape, 1)
    parts[me] = jnp.zeros(parts.shape[1:], jnp.float32)
    parts[me, :, 0 : F + R] = jnp.where(kind < F, part_points, part_weights)

    def part_copy(index):
        return send(
            parts.at[me],
            parts.at[me],
            part_send.at[index],
            part_recv.at[me],
            (me + 1 + index) % n,
        )

    def part_arrived(index):
        other = (me + 1 + index) % n
        send(
            parts.at[other], parts.at[other], part_send.at[index], part_recv.at[other], other
        ).wait_recv()

    each(n - 1, lambda index: part_copy(index).start())

    group_of = lax.broadcasted_iota(jnp.int32, (R, cluster * quarter), 1) // S
    side_weights = jnp.where(group_of != group_in_cluster, stack[F : F + R, :], 0.0)
    side = far_sum(side_weights, stack[0:F, columns_of(group_in_cluster)], stack[0:F, :])

    each(n - 1, part_arrived)
    parts_turned[...] = parts[...].reshape(n * part, parts.shape[2]).T
    own_cluster = me // cluster
    cluster_of = lax.broadcasted_iota(jnp.int32, (R, n * part), 1) // S
    top_weights = jnp.where(cluster_of != own_cluster, parts_turned[F : F + R, :], 0.0)
    top = far_sum(top_weights, parts_turned[0:F, columns_of(own_cluster)], parts_turned[0:F, :])

    def hand_on(index):
        slot = index * 2

        @pl.when((index != REACH // 2) & inside(me + slot - middle_slot))
        def _():
            arrived(slot)

            @pl.when(forwarded(index))
            def _():
                forward_copy(index).start()

    each(REACH + 1, hand_on)

    def rows_arrived(index):
        other = (child + 1 + index) % group
        send(
            group_rows.at[other],
            group_rows.at[other],
            rows_send.at[index],
            rows_recv.at[other],
            group_first + other,
        ).wait_recv()

    def cluster_rows_arrived(index):
        other = (place + 1 + index) % cluster
        send(
            cluster_rows.at[other],
            cluster_rows.at[other],
            cluster_rows_send.at[index],
            cluster_rows_recv.at[other],
            cluster_first + other,
        ).wait_recv()

    each(group - 1, rows_arrived)
    each(cluster - 1, cluster_rows_arrived)

    down_group = side + product(top, cluster_rows[...].reshape(cluster * part, S), 0)
    down_device = product(down_group, group_rows[...].reshape(group * quarter, S), 0)
    for inner in range(LEAVES_DEV):
        rows = slice(inner * leaf, (inner + 1) * leaf)
        down_leaf = product(down_device, device_basis[inner * S : (inner + 1) * S, :], 1)
        far[:, rows] = product(down_leaf, leaf_basis[rows, :], 1)

    def landed(index):
        slot = index * 2 + 1

        @pl.when(inside(me + slot - middle_slot))
        def _():
            arrived(slot)

    each(REACH, landed)

    def lane_sent(index):
        @pl.when(inside(me + lane_offset(index)))
        def _():
            lane_copy(index).wait_send()

    def forward_sent(index):
        @pl.when(forwarded(index))
        def _():
            forward_copy(index).wait_send()

    each(REACH, lane_sent)
    each(REACH + 1, forward_sent)
    each(group - 1, lambda index: group_rows_copy(index).wait_send())
    each(cluster - 1, lambda index: cluster_rows_copy(index).wait_send())
    each(group - 1, lambda index: device_copy(index).wait_send())
    each(cluster - 1, lambda index: quarter_copy(index).wait_send())
    each(n - 1, lambda index: part_copy(index).wait_send())


def tree(points, charges, leaf_basis, device_basis, device_skeleton, group_basis, group_skeleton,
         cluster_basis, cluster_skeleton):
    n = lax.axis_size("leaf")
    quarter, part = group_basis.shape[1], cluster_basis.shape[1]
    group, cluster = S // quarter, S // part
    width = points.shape[1]
    vmem = pl.BlockSpec(memory_space=pltpu.VMEM)
    dma = pltpu.SemaphoreType.DMA
    return pl.pallas_call(
        functools.partial(tree_kernel, n),
        out_shape=(
            jax.ShapeDtypeStruct((2 * REACH + 1, F + R, width), jnp.float32),
            jax.ShapeDtypeStruct((R, width), jnp.float32),
        ),
        in_specs=[vmem] * 9,
        out_specs=(pl.BlockSpec(memory_space=pl.ANY), vmem),
        scratch_shapes=[
            pltpu.VMEM((quarter, group * S), jnp.float32),
            pltpu.VMEM((part, group * S), jnp.float32),
            pltpu.VMEM((group, quarter, S), jnp.float32),
            pltpu.VMEM((cluster, part, S), jnp.float32),
            pltpu.VMEM((group, F + R, S), jnp.float32),
            pltpu.VMEM((cluster, F, 2 * quarter), jnp.float32),
            pltpu.VMEM((F + R, cluster * quarter), jnp.float32),
            pltpu.VMEM((n, part, 128), jnp.float32),
            pltpu.VMEM((128, n * part), jnp.float32),
            dma((2,)),
            dma((REACH,)),
            dma((REACH + 1,)),
            dma((2 * REACH + 1,)),
            dma((group - 1,)),
            dma((group,)),
            dma((cluster - 1,)),
            dma((cluster,)),
            dma((group - 1,)),
            dma((group,)),
            dma((cluster - 1,)),
            dma((cluster,)),
            dma((n - 1,)),
            dma((n,)),
        ],
        compiler_params=pltpu.CompilerParams(
            collective_id=0, has_side_effects=True, vmem_limit_bytes=48 * 1024 * 1024
        ),
        name="tree_and_window",
    )(
        points,
        charges,
        leaf_basis,
        device_basis,
        device_skeleton,
        group_basis,
        group_skeleton[None, :],
        cluster_basis,
        cluster_skeleton[:, None],
    )


def shards(points, charges, near_list, near_count, leaf_basis, device_basis, device_skeleton,
           group_basis, group_skeleton, cluster_basis, cluster_skeleton):
    window, far = tree(points, charges, leaf_basis, device_basis, device_skeleton, group_basis,
                       group_skeleton, cluster_basis, cluster_skeleton)
    return near_field(points, window, near_list, near_count, far)


def solution(mesh):
    return jax.shard_map(
        shards,
        mesh=mesh,
        in_specs=(
            P(None, "leaf"),
            P(None, "leaf"),
            P("leaf", None),
            P("leaf"),
            P("leaf", None),
            P("leaf", None),
            P("leaf", None),
            P(None, "leaf"),
            P("leaf"),
            P(None, "leaf"),
            P("leaf"),
        ),
        out_specs=P(None, "leaf"),
        check_vma=False,
    )
```

```python
import functools
import math

import jax
import jax.numpy as jnp
from jax import lax
from jax.experimental import pallas as pl
from jax.experimental.pallas import tpu as pltpu
from jax.sharding import PartitionSpec as P

F = 16
R = 16
S = 256
REACH = 8
LEAVES_DEV = 4
VMEM_BYTES = 60 * 1024 * 1024


inverse_spread = 1.0 / 16.0


def split3(value):
    high = value.astype(jnp.bfloat16)
    rest = value - high.astype(jnp.float32)
    middle = rest.astype(jnp.bfloat16)
    low = (rest - middle.astype(jnp.float32)).astype(jnp.bfloat16)
    return high, middle, low


def norm_rows(squares, first):
    high, middle, low = (piece.astype(jnp.float32) for piece in split3(squares))
    row = lax.broadcasted_iota(jnp.int32, (16, squares.shape[1]), 0)
    ones = 3 - first
    block = jnp.where((row >= ones) & (row < ones + 3), 1.0, 0.0)
    block = jnp.where(row == first, high, block)
    block = jnp.where(row == first + 1, middle, block)
    return jnp.where(row == first + 2, low, block)


def split2(value):
    high = value.astype(jnp.bfloat16)
    return high, (value - high.astype(jnp.float32)).astype(jnp.bfloat16)


def product(left, right, contract):
    dims = (((1,), (contract,)), ((), ()))
    left_high, left_low = split2(left)
    right_high, right_low = split2(right)
    rows = left.shape[0]
    both = lax.dot_general(
        jnp.concatenate([left_high, left_low], axis=0),
        right_high,
        dims,
        preferred_element_type=jnp.float32,
    )
    rest = lax.dot_general(left_high, right_low, dims, preferred_element_type=jnp.float32)
    return both[:rows] + (both[rows:] + rest)


def pick(values, one_hot):
    stacked = jnp.concatenate(list(split3(values)), axis=0)
    picked = jnp.dot(stacked, one_hot, preferred_element_type=jnp.float32)
    rows = values.shape[0]
    return picked[:rows] + picked[rows : 2 * rows] + picked[2 * rows :]


def source_rows(block):
    scale = inverse_spread * math.log2(math.e)
    high, middle, low = split3(block)
    squares = jnp.sum(block * block, axis=0, keepdims=True) * (-scale)
    norms = norm_rows(squares, 3).astype(jnp.bfloat16)
    return (high, middle, high, low, high, middle, norms, jnp.zeros_like(norms))


def target_rows(block):
    scale = inverse_spread * math.log2(math.e)
    high, middle, low = (p.astype(jnp.float32) for p in split3(block * (2.0 * scale)))
    squares = jnp.sum(block * block, axis=0, keepdims=True) * (-scale)
    norms = norm_rows(squares, 0)
    stacked = jnp.concatenate(
        [high, high, middle, high, low, middle, norms, jnp.zeros_like(norms)], axis=0
    )
    return stacked.T.astype(jnp.bfloat16)


def far_sum(weights, targets, sources):
    power = jnp.dot(
        target_rows(targets),
        jnp.concatenate(list(source_rows(sources)), axis=0),
        preferred_element_type=jnp.float32,
    )
    return product(weights, jnp.exp2(power), 1)


def one_hot_of(indices, rows, first):
    row = lax.broadcasted_iota(jnp.int32, (rows, indices.shape[1]), 0) + first
    return (row == indices).astype(jnp.float32).astype(jnp.bfloat16)


def near_kernel(
    list_ref, count_ref, window_ref, far_ref, out_ref, window, source, charge, target, total, sems
):
    devices, _, width = window.shape
    leaf = source.shape[2]
    leaves_dev = width // leaf
    first_leaf = (lax.axis_index("leaf") - REACH) * leaves_dev

    def block_copy(device):
        return pltpu.make_async_copy(window_ref.at[device], window.at[device], sems.at[device])

    def fetch(device, carry):
        block_copy(device).start()
        return carry

    lax.fori_loop(0, devices, fetch, 0)

    def prepare(device, carry):
        block_copy(device).wait()
        for inner in range(leaves_dev):
            columns = slice(inner * leaf, (inner + 1) * leaf)
            slot = device * leaves_dev + inner
            for place, piece in enumerate(source_rows(window[device, 0:F, columns])):
                source[slot, place * 16 : (place + 1) * 16, :] = piece
            charge[slot] = window[device, F : F + R, columns].astype(jnp.bfloat16)
        return carry

    lax.fori_loop(0, devices, prepare, 0)

    for inner in range(leaves_dev):
        columns = slice(inner * leaf, (inner + 1) * leaf)
        target[...] = target_rows(window[REACH, 0:F, columns])
        total[...] = jnp.zeros_like(total)
        count = count_ref[inner]

        def two_tiles(step, carry):
            tiles, weights = [], []
            for side in range(2):
                slot = step * 2 + side
                picked = list_ref[inner, slot] - first_leaf
                live = (slot < count).astype(jnp.float32)
                power = jnp.dot(target[...], source[picked], preferred_element_type=jnp.float32)
                tiles.append(jnp.exp2(power).astype(jnp.bfloat16))
                weights.append((charge[picked].astype(jnp.float32) * live).astype(jnp.bfloat16))
            total[...] += lax.dot_general(
                jnp.concatenate(tiles, axis=1),
                jnp.concatenate(weights, axis=1),
                (((1,), (1,)), ((), ())),
                preferred_element_type=jnp.float32,
            )
            return carry

        lax.fori_loop(0, (count + 1) // 2, two_tiles, 0)
        out_ref[:, columns] = total[...].T + far_ref[:, columns]


def near_field(window, near_list, near_count, far):
    devices, rows, width = window.shape
    leaves_dev = near_list.shape[0]
    leaf = width // leaves_dev
    slots = devices * leaves_dev
    vmem = pl.BlockSpec(memory_space=pltpu.VMEM)
    smem = pl.BlockSpec(memory_space=pltpu.SMEM)
    return pl.pallas_call(
        near_kernel,
        out_shape=jax.ShapeDtypeStruct((R, width), jnp.float32),
        in_specs=[smem, smem, pl.BlockSpec(memory_space=pl.ANY), vmem],
        out_specs=vmem,
        scratch_shapes=[
            pltpu.VMEM((devices, rows, width), jnp.float32),
            pltpu.VMEM((slots, 128, leaf), jnp.bfloat16),
            pltpu.VMEM((slots, R, leaf), jnp.bfloat16),
            pltpu.VMEM((leaf, 128), jnp.bfloat16),
            pltpu.VMEM((leaf, R), jnp.float32),
            pltpu.SemaphoreType.DMA((devices,)),
        ],
        compiler_params=pltpu.CompilerParams(vmem_limit_bytes=VMEM_BYTES),
        name="near_tiles",
    )(near_list, near_count, window, far)


def tree_kernel(
    n,
    points_in,
    charges_in,
    leaf_basis_in,
    device_basis_in,
    device_skeleton_in,
    group_basis_in,
    group_skeleton_in,
    cluster_basis_in,
    cluster_skeleton_in,
    window,
    far,
    points,
    charges,
    leaf_basis,
    device_basis,
    device_skeleton,
    group_own,
    group_skeleton,
    cluster_own,
    cluster_skeleton,
    group_rows,
    cluster_rows,
    device_nodes,
    quarters,
    stack,
    parts,
    parts_turned,
    local_sem,
    window_send,
    forward_send,
    window_recv,
    rows_send,
    rows_recv,
    cluster_rows_send,
    cluster_rows_recv,
    device_send,
    device_recv,
    quarter_send,
    quarter_recv,
    part_send,
    part_recv,
):
    me = lax.axis_index("leaf")
    group = device_nodes.shape[0]
    cluster = quarters.shape[0]
    quarter = group_own.shape[0]
    part = cluster_own.shape[0]
    leaf = points.shape[1] // LEAVES_DEV
    place, child = me % cluster, me % group
    group_first, cluster_first = me - child, me - place
    group_in_cluster = place // group
    core = me % 2
    sibling = me + 1 - 2 * core
    middle_slot = REACH
    last = REACH - 1
    first_sends = (0, last)
    second_sends = tuple(range(REACH // 4, REACH - REACH // 4))
    third_sends = tuple(i for i in range(1, last) if i not in second_sends)
    late_slots = tuple(i if i < REACH // 2 else i + 1 for i in third_sends)
    early_slots = tuple(i for i in range(REACH + 1) if i not in late_slots)

    def send(source, destination, send_sem, recv_sem, device):
        return pltpu.make_async_remote_copy(
            src_ref=source,
            dst_ref=destination,
            send_sem=send_sem,
            recv_sem=recv_sem,
            device_id=(device,),
            device_id_type=pl.DeviceIdType.MESH,
        )

    def each(count, body):
        def step(index, carry):
            body(index)
            return carry

        lax.fori_loop(0, count, step, 0)

    def columns_of(index):
        return pl.ds(pl.multiple_of(index * S, S), S)

    barrier = pltpu.get_barrier_semaphore()

    def greet(index):
        other = (me + 1 + index) % n
        pl.semaphore_signal(
            barrier, inc=1, device_id=(other,), device_id_type=pl.DeviceIdType.MESH
        )

    each(n - 1, greet)
    fetched = [
        (points_in, points),
        (device_skeleton_in, device_skeleton),
        (charges_in, charges),
        (leaf_basis_in, leaf_basis),
        (device_basis_in, device_basis),
        (group_basis_in, group_own),
        (group_skeleton_in, group_skeleton),
        (cluster_basis_in, cluster_own),
        (cluster_skeleton_in, cluster_skeleton),
        (points_in, window.at[middle_slot, pl.ds(0, F)]),
        (charges_in, window.at[middle_slot, pl.ds(F, R)]),
    ]
    fetches = [
        pltpu.make_async_copy(here, there, local_sem.at[index])
        for index, (here, there) in enumerate(fetched)
    ]
    for index in (0, 1, 9, 10, 2, 3, 4, 5, 6, 7, 8):
        fetches[index].start()

    def lane_offset(index):
        return jnp.where(index < REACH // 2, index - REACH // 2, index - REACH // 2 + 1) * 2

    def lane_copy(index):
        offset = lane_offset(index)
        slot = middle_slot - offset
        return send(
            window.at[middle_slot],
            window.at[slot],
            window_send.at[index],
            window_recv.at[slot],
            jnp.clip(me + offset, 0, n - 1),
        )

    def inside(device):
        return (device >= 0) & (device < n)

    def start_lane(index):
        @pl.when(inside(me + lane_offset(index)))
        def _():
            lane_copy(index).start()

    def forward_copy(index):
        slot = index * 2
        landing = jnp.clip(slot - 1 + 2 * core, 0, 2 * REACH)
        return send(
            window.at[slot],
            window.at[landing],
            forward_send.at[index],
            window_recv.at[landing],
            sibling,
        )

    def forwarded(index):
        slot = index * 2
        landing = slot - 1 + 2 * core
        return inside(me + slot - middle_slot) & (landing >= 0) & (landing <= 2 * REACH)

    def arrived(slot):
        send(
            window.at[slot], window.at[slot], window_send.at[0], window_recv.at[slot], sibling
        ).wait_recv()

    fetches[0].wait()
    fetches[1].wait()
    device_points = jnp.zeros((F, S), jnp.float32)
    for inner in range(LEAVES_DEV):
        rows = slice(inner * leaf, (inner + 1) * leaf)
        device_points += pick(
            points[:, rows], one_hot_of(device_skeleton[...], leaf, inner * leaf)
        )
    device_nodes[child, 0:F, :] = device_points
    for index in range(2, len(fetches)):
        fetches[index].wait()
    pl.semaphore_wait(barrier, n - 1)
    for index in first_sends:
        start_lane(index)
    forward_copy(REACH // 2).start()

    def group_rows_copy(index):
        other = (child + 1 + index) % group
        return send(
            group_own.at[:, columns_of(other)],
            group_rows.at[child],
            rows_send.at[index],
            rows_recv.at[child],
            group_first + other,
        )

    def cluster_rows_copy(index):
        other = (place + 1 + index) % cluster
        return send(
            cluster_own.at[:, columns_of(other // group)],
            cluster_rows.at[place],
            cluster_rows_send.at[index],
            cluster_rows_recv.at[place],
            cluster_first + other,
        )

    device_weights = jnp.zeros((R, S), jnp.float32)
    for inner in range(LEAVES_DEV):
        rows = slice(inner * leaf, (inner + 1) * leaf)
        leaf_weights = product(charges[:, rows], leaf_basis[rows, :], 0)
        device_weights += product(
            leaf_weights, device_basis[inner * S : (inner + 1) * S, :], 0
        )
    device_nodes[child, F : F + R, :] = device_weights

    def device_copy(index):
        other = (child + 1 + index) % group
        return send(
            device_nodes.at[child],
            device_nodes.at[child],
            device_send.at[index],
            device_recv.at[child],
            group_first + other,
        )

    def device_arrived(index):
        other = (child + 1 + index) % group
        send(
            device_nodes.at[other],
            device_nodes.at[other],
            device_send.at[index],
            device_recv.at[other],
            group_first + other,
        ).wait_recv()

    each(group - 1, lambda index: device_copy(index).start())
    for index in second_sends:
        start_lane(index)
    each(group - 1, lambda index: group_rows_copy(index).start())
    each(cluster - 1, lambda index: cluster_rows_copy(index).start())
    group_rows[child] = group_own[:, columns_of(child)]
    cluster_rows[place] = cluster_own[:, columns_of(group_in_cluster)]
    each(group - 1, device_arrived)

    quarter_weights = jnp.zeros((R, quarter), jnp.float32)
    quarter_points = jnp.zeros((F, quarter), jnp.float32)
    for inner in range(group):
        quarter_weights += product(
            device_nodes[inner, F : F + R, :], group_own[:, inner * S : (inner + 1) * S], 1
        )
        quarter_points += pick(
            device_nodes[inner, 0:F, :], one_hot_of(group_skeleton[...], S, inner * S)
        )
    quarters[place] = jnp.concatenate([quarter_points, quarter_weights], axis=1)

    def quarter_copy(index):
        other = (place + 1 + index) % cluster
        return send(
            quarters.at[place],
            quarters.at[place],
            quarter_send.at[index],
            quarter_recv.at[place],
            cluster_first + other,
        )

    def quarter_arrived(index):
        other = (place + 1 + index) % cluster
        send(
            quarters.at[other],
            quarters.at[other],
            quarter_send.at[index],
            quarter_recv.at[other],
            cluster_first + other,
        ).wait_recv()

    each(cluster - 1, lambda index: quarter_copy(index).start())
    for index in third_sends:
        start_lane(index)
    each(cluster - 1, quarter_arrived)

    lane = lax.broadcasted_iota(jnp.int32, (F, 2 * quarter), 1)
    for pair in range(cluster // 2):
        even, odd = quarters[2 * pair], quarters[2 * pair + 1]
        columns = slice(pair * 2 * quarter, (pair + 1) * 2 * quarter)
        stack[0:F, columns] = jnp.where(lane < quarter, even, pltpu.roll(odd, quarter, 1))
        stack[F : F + R, columns] = jnp.where(lane < quarter, pltpu.roll(even, quarter, 1), odd)

    part_points = jnp.zeros((F, part), jnp.float32)
    for inner in range(group):
        part_points += pick(
            stack[0:F, inner * S : (inner + 1) * S],
            one_hot_of(cluster_skeleton[...], S, inner * S),
        )
    part_weights = product(stack[F : F + R, :], cluster_own[...], 1)
    node_rows = jnp.concatenate(
        [part_points, part_weights, jnp.zeros((128 - F - R, part), jnp.float32)], axis=0
    ).T
    parts[me] = node_rows[: part // 2] + pltpu.roll(node_rows[part // 2 :], F + R, 1)

    def part_copy(index):
        return send(
            parts.at[me],
            parts.at[me],
            part_send.at[index],
            part_recv.at[me],
            (me + 1 + index) % n,
        )

    def part_arrived(index):
        other = (me + 1 + index) % n
        send(
            parts.at[other], parts.at[other], part_send.at[index], part_recv.at[other], other
        ).wait_recv()

    each(n - 1, lambda index: part_copy(index).start())

    group_of = lax.broadcasted_iota(jnp.int32, (R, cluster * quarter), 1) // S
    side_weights = jnp.where(group_of != group_in_cluster, stack[F : F + R, :], 0.0)
    side = far_sum(side_weights, stack[0:F, columns_of(group_in_cluster)], stack[0:F, :])

    def hand_on(index):
        slot = index * 2

        @pl.when(inside(me + slot - middle_slot))
        def _():
            arrived(slot)

            @pl.when(forwarded(index))
            def _():
                forward_copy(index).start()

    for index in early_slots:
        if index != REACH // 2:
            hand_on(index)

    each(n - 1, part_arrived)
    half = part // 2
    parts_turned[...] = parts[...].reshape(n * half, parts.shape[2]).T
    own_columns = pl.ds(pl.multiple_of((me // cluster) * cluster * half, cluster * half), cluster * half)
    cluster_of = lax.broadcasted_iota(jnp.int32, (R, n * half), 1) // (cluster * half)
    others = cluster_of != me // cluster
    upper = F + R
    all_points = jnp.concatenate(
        [parts_turned[0:F, :], parts_turned[upper : upper + F, :]], axis=1
    )
    all_weights = jnp.concatenate(
        [
            jnp.where(others, parts_turned[F:upper, :], 0.0),
            jnp.where(others, parts_turned[upper + F : upper + F + R, :], 0.0),
        ],
        axis=1,
    )
    own_points = jnp.concatenate(
        [parts_turned[0:F, own_columns], parts_turned[upper : upper + F, own_columns]], axis=1
    )
    top = far_sum(all_weights, own_points, all_points)

    for index in late_slots:
        hand_on(index)

    def rows_arrived(index):
        other = (child + 1 + index) % group
        send(
            group_rows.at[other],
            group_rows.at[other],
            rows_send.at[index],
            rows_recv.at[other],
            group_first + other,
        ).wait_recv()

    def cluster_rows_arrived(index):
        other = (place + 1 + index) % cluster
        send(
            cluster_rows.at[other],
            cluster_rows.at[other],
            cluster_rows_send.at[index],
            cluster_rows_recv.at[other],
            cluster_first + other,
        ).wait_recv()

    each(group - 1, rows_arrived)
    each(cluster - 1, cluster_rows_arrived)

    rows_of_cluster = jnp.concatenate(
        [
            cluster_rows[:, :half, :].reshape(cluster * half, S),
            cluster_rows[:, half:, :].reshape(cluster * half, S),
        ],
        axis=0,
    )
    down_group = side + product(top, rows_of_cluster, 0)
    down_device = product(down_group, group_rows[...].reshape(group * quarter, S), 0)
    for inner in range(LEAVES_DEV):
        rows = slice(inner * leaf, (inner + 1) * leaf)
        down_leaf = product(down_device, device_basis[inner * S : (inner + 1) * S, :], 1)
        far[:, rows] = product(down_leaf, leaf_basis[rows, :], 1)

    def landed(index):
        slot = index * 2 + 1

        @pl.when(inside(me + slot - middle_slot))
        def _():
            arrived(slot)

    each(REACH, landed)

    def lane_sent(index):
        @pl.when(inside(me + lane_offset(index)))
        def _():
            lane_copy(index).wait_send()

    def forward_sent(index):
        @pl.when(forwarded(index))
        def _():
            forward_copy(index).wait_send()

    each(REACH, lane_sent)
    each(REACH + 1, forward_sent)
    each(group - 1, lambda index: group_rows_copy(index).wait_send())
    each(cluster - 1, lambda index: cluster_rows_copy(index).wait_send())
    each(group - 1, lambda index: device_copy(index).wait_send())
    each(cluster - 1, lambda index: quarter_copy(index).wait_send())
    each(n - 1, lambda index: part_copy(index).wait_send())


def tree(points, charges, leaf_basis, device_basis, device_skeleton, group_basis, group_skeleton,
         cluster_basis, cluster_skeleton):
    n = lax.axis_size("leaf")
    quarter, part = group_basis.shape[1], cluster_basis.shape[1]
    group, cluster = S // quarter, S // part
    width = points.shape[1]
    vmem = pl.BlockSpec(memory_space=pltpu.VMEM)
    dma = pltpu.SemaphoreType.DMA
    return pl.pallas_call(
        functools.partial(tree_kernel, n),
        out_shape=(
            jax.ShapeDtypeStruct((2 * REACH + 1, F + R, width), jnp.float32),
            jax.ShapeDtypeStruct((R, width), jnp.float32),
        ),
        in_specs=[pl.BlockSpec(memory_space=pl.ANY)] * 9,
        out_specs=(pl.BlockSpec(memory_space=pl.ANY), vmem),
        scratch_shapes=[
            pltpu.VMEM(points.shape, jnp.float32),
            pltpu.VMEM(charges.shape, jnp.float32),
            pltpu.VMEM(leaf_basis.shape, jnp.float32),
            pltpu.VMEM(device_basis.shape, jnp.float32),
            pltpu.VMEM(device_skeleton.shape, jnp.int32),
            pltpu.VMEM((quarter, group * S), jnp.float32),
            pltpu.VMEM((1, quarter), jnp.int32),
            pltpu.VMEM((part, group * S), jnp.float32),
            pltpu.VMEM((1, part), jnp.int32),
            pltpu.VMEM((group, quarter, S), jnp.float32),
            pltpu.VMEM((cluster, part, S), jnp.float32),
            pltpu.VMEM((group, F + R, S), jnp.float32),
            pltpu.VMEM((cluster, F, 2 * quarter), jnp.float32),
            pltpu.VMEM((F + R, cluster * quarter), jnp.float32),
            pltpu.VMEM((n, part // 2, 128), jnp.float32),
            pltpu.VMEM((128, n * part // 2), jnp.float32),
            dma((11,)),
            dma((REACH,)),
            dma((REACH + 1,)),
            dma((2 * REACH + 1,)),
            dma((group - 1,)),
            dma((group,)),
            dma((cluster - 1,)),
            dma((cluster,)),
            dma((group - 1,)),
            dma((group,)),
            dma((cluster - 1,)),
            dma((cluster,)),
            dma((n - 1,)),
            dma((n,)),
        ],
        compiler_params=pltpu.CompilerParams(
            collective_id=0, has_side_effects=True, vmem_limit_bytes=VMEM_BYTES
        ),
        name="tree_and_window",
    )(
        points,
        charges,
        leaf_basis,
        device_basis,
        device_skeleton,
        group_basis.T,
        group_skeleton[None, :],
        cluster_basis.T,
        cluster_skeleton[None, :],
    )


def shards(points, charges, near_list, near_count, leaf_basis, device_basis, device_skeleton,
           group_basis, group_skeleton, cluster_basis, cluster_skeleton):
    window, far = tree(points, charges, leaf_basis, device_basis, device_skeleton, group_basis,
                       group_skeleton, cluster_basis, cluster_skeleton)
    return near_field(window, near_list, near_count, far)


def solution(mesh):
    return jax.shard_map(
        shards,
        mesh=mesh,
        in_specs=(
            P(None, "leaf"),
            P(None, "leaf"),
            P("leaf", None),
            P("leaf"),
            P("leaf", None),
            P("leaf", None),
            P("leaf", None),
            P(None, "leaf"),
            P("leaf"),
            P(None, "leaf"),
            P("leaf"),
        ),
        out_specs=P(None, "leaf"),
        check_vma=False,
    )
```

```python
import functools
import math

import jax
import jax.numpy as jnp
from jax import lax
from jax.experimental import pallas as pl
from jax.experimental.pallas import tpu as pltpu
from jax.sharding import PartitionSpec as P

F = 16
R = 16
S = 256
REACH = 8
LEAVES_DEV = 4
VMEM_BYTES = 60 * 1024 * 1024


inverse_spread = 1.0 / 16.0


def split3(value):
    high = value.astype(jnp.bfloat16)
    rest = value - high.astype(jnp.float32)
    middle = rest.astype(jnp.bfloat16)
    low = (rest - middle.astype(jnp.float32)).astype(jnp.bfloat16)
    return high, middle, low


def norm_rows(squares, first):
    high, middle, low = (piece.astype(jnp.float32) for piece in split3(squares))
    row = lax.broadcasted_iota(jnp.int32, (16, squares.shape[1]), 0)
    ones = 3 - first
    block = jnp.where((row >= ones) & (row < ones + 3), 1.0, 0.0)
    block = jnp.where(row == first, high, block)
    block = jnp.where(row == first + 1, middle, block)
    return jnp.where(row == first + 2, low, block)


def split2(value):
    high = value.astype(jnp.bfloat16)
    return high, (value - high.astype(jnp.float32)).astype(jnp.bfloat16)


def product(left, right, contract):
    dims = (((1,), (contract,)), ((), ()))
    left_high, left_low = split2(left)
    right_high, right_low = split2(right)
    rows = left.shape[0]
    both = lax.dot_general(
        jnp.concatenate([left_high, left_low], axis=0),
        right_high,
        dims,
        preferred_element_type=jnp.float32,
    )
    rest = lax.dot_general(left_high, right_low, dims, preferred_element_type=jnp.float32)
    return both[:rows] + (both[rows:] + rest)


def pick(values, one_hot):
    stacked = jnp.concatenate(list(split3(values)), axis=0)
    picked = jnp.dot(stacked, one_hot, preferred_element_type=jnp.float32)
    rows = values.shape[0]
    return picked[:rows] + picked[rows : 2 * rows] + picked[2 * rows :]


def source_rows(block):
    scale = inverse_spread * math.log2(math.e)
    high, middle, low = split3(block)
    squares = jnp.sum(block * block, axis=0, keepdims=True) * (-scale)
    norms = norm_rows(squares, 3).astype(jnp.bfloat16)
    return (high, middle, high, low, high, middle, norms, jnp.zeros_like(norms))


def target_rows(block):
    scale = inverse_spread * math.log2(math.e)
    high, middle, low = (p.astype(jnp.float32) for p in split3(block * (2.0 * scale)))
    squares = jnp.sum(block * block, axis=0, keepdims=True) * (-scale)
    norms = norm_rows(squares, 0)
    stacked = jnp.concatenate(
        [high, high, middle, high, low, middle, norms, jnp.zeros_like(norms)], axis=0
    )
    return stacked.T.astype(jnp.bfloat16)


def far_sum(weights, targets, sources):
    power = jnp.dot(
        target_rows(targets),
        jnp.concatenate(list(source_rows(sources)), axis=0),
        preferred_element_type=jnp.float32,
    )
    return product(weights, jnp.exp2(power), 1)


def one_hot_of(indices, rows, first):
    row = lax.broadcasted_iota(jnp.int32, (rows, indices.shape[1]), 0) + first
    return (row == indices).astype(jnp.float32).astype(jnp.bfloat16)


def near_kernel(
    list_ref,
    count_ref,
    window_ref,
    far_ref,
    out_ref,
    window,
    source,
    charge,
    target,
    power,
    tile,
    total,
    plan_leaf,
    plan_source,
    sems,
):
    devices, _, width = window.shape
    leaf = source.shape[2]
    leaves_dev = width // leaf
    first_leaf = (lax.axis_index("leaf") - REACH) * leaves_dev

    def block_copy(device):
        return pltpu.make_async_copy(window_ref.at[device], window.at[device], sems.at[device])

    def fetch(device, carry):
        block_copy(device).start()
        return carry

    lax.fori_loop(0, devices, fetch, 0)

    def prepare(device, carry):
        block_copy(device).wait()
        for inner in range(leaves_dev):
            columns = slice(inner * leaf, (inner + 1) * leaf)
            slot = device * leaves_dev + inner
            for place, piece in enumerate(source_rows(window[device, 0:F, columns])):
                source[slot, place * 16 : (place + 1) * 16, :] = piece
            charge[slot] = window[device, F : F + R, columns].astype(jnp.bfloat16)
        return carry

    lax.fori_loop(0, devices, prepare, 0)

    end = jnp.int32(0)
    for inner in range(leaves_dev):
        columns = slice(inner * leaf, (inner + 1) * leaf)
        target[inner] = target_rows(window[REACH, 0:F, columns])
        total[inner] = jnp.zeros(total.shape[1:], jnp.float32)

        def enter(slot, place, inner=inner):
            plan_leaf[place] = inner
            plan_source[place] = list_ref[inner, slot] - first_leaf
            return place + 1

        end = lax.fori_loop(0, count_ref[inner], enter, end)
    power[...] = jnp.zeros_like(power)
    tile[...] = jnp.zeros_like(tile)

    def step(index, carry):
        done = jnp.clip(index - 2, 0, end - 1)
        live = (index >= 2).astype(jnp.float32)
        weights = (charge[plan_source[done]].astype(jnp.float32) * live).astype(jnp.bfloat16)
        total[plan_leaf[done]] += lax.dot_general(
            weights, tile[...], (((1,), (1,)), ((), ())), preferred_element_type=jnp.float32
        )
        tile[...] = jnp.exp2(power[...]).astype(jnp.bfloat16)
        fresh = jnp.minimum(index, end - 1)
        power[...] = jnp.dot(
            target[plan_leaf[fresh]], source[plan_source[fresh]], preferred_element_type=jnp.float32
        )
        return carry

    lax.fori_loop(0, end + 2, step, 0)
    for inner in range(leaves_dev):
        columns = slice(inner * leaf, (inner + 1) * leaf)
        out_ref[:, columns] = total[inner] + far_ref[:, columns]


def near_field(window, near_list, near_count, far):
    devices, rows, width = window.shape
    leaves_dev = near_list.shape[0]
    leaf = width // leaves_dev
    slots = devices * leaves_dev
    vmem = pl.BlockSpec(memory_space=pltpu.VMEM)
    smem = pl.BlockSpec(memory_space=pltpu.SMEM)
    return pl.pallas_call(
        near_kernel,
        out_shape=jax.ShapeDtypeStruct((R, width), jnp.float32),
        in_specs=[smem, smem, pl.BlockSpec(memory_space=pl.ANY), vmem],
        out_specs=vmem,
        scratch_shapes=[
            pltpu.VMEM((devices, rows, width), jnp.float32),
            pltpu.VMEM((slots, 128, leaf), jnp.bfloat16),
            pltpu.VMEM((slots, R, leaf), jnp.bfloat16),
            pltpu.VMEM((leaves_dev, leaf, 128), jnp.bfloat16),
            pltpu.VMEM((leaf, leaf), jnp.float32),
            pltpu.VMEM((leaf, leaf), jnp.bfloat16),
            pltpu.VMEM((leaves_dev, R, leaf), jnp.float32),
            pltpu.SMEM((near_list.size,), jnp.int32),
            pltpu.SMEM((near_list.size,), jnp.int32),
            pltpu.SemaphoreType.DMA((devices,)),
        ],
        compiler_params=pltpu.CompilerParams(vmem_limit_bytes=VMEM_BYTES),
        name="near_tiles",
    )(near_list, near_count, window, far)


def tree_kernel(
    n,
    points_in,
    charges_in,
    leaf_basis_in,
    device_basis_in,
    device_skeleton_in,
    group_basis_in,
    group_skeleton_in,
    cluster_basis_in,
    cluster_skeleton_in,
    window,
    far,
    points,
    charges,
    leaf_basis,
    device_basis,
    device_skeleton,
    group_own,
    group_skeleton,
    cluster_own,
    cluster_skeleton,
    group_rows,
    cluster_rows,
    device_nodes,
    quarters,
    stack,
    parts,
    parts_turned,
    local_sem,
    window_send,
    forward_send,
    window_recv,
    rows_send,
    rows_recv,
    cluster_rows_send,
    cluster_rows_recv,
    device_send,
    device_recv,
    quarter_send,
    quarter_recv,
    part_send,
    part_recv,
):
    me = lax.axis_index("leaf")
    group = device_nodes.shape[0]
    cluster = quarters.shape[0]
    quarter = group_own.shape[0]
    part = cluster_own.shape[0]
    leaf = points.shape[1] // LEAVES_DEV
    place, child = me % cluster, me % group
    group_first, cluster_first = me - child, me - place
    group_in_cluster = place // group
    core = me % 2
    sibling = me + 1 - 2 * core
    middle_slot = REACH
    last = REACH - 1
    first_sends = (0, last)
    second_sends = tuple(range(REACH // 4, REACH - REACH // 4))
    third_sends = tuple(i for i in range(1, last) if i not in second_sends)
    late_slots = tuple(i if i < REACH // 2 else i + 1 for i in third_sends)
    early_slots = tuple(i for i in range(REACH + 1) if i not in late_slots)

    def send(source, destination, send_sem, recv_sem, device):
        return pltpu.make_async_remote_copy(
            src_ref=source,
            dst_ref=destination,
            send_sem=send_sem,
            recv_sem=recv_sem,
            device_id=(device,),
            device_id_type=pl.DeviceIdType.MESH,
        )

    def around(position, index, size):
        other = position + 1 + index
        return jnp.where(other >= size, other - size, other)

    def all_of(ref, send_sem, recv_sem):
        return send(ref, ref, send_sem, recv_sem, sibling)

    def each(count, body):
        def step(index, carry):
            body(index)
            return carry

        lax.fori_loop(0, count, step, 0)

    def columns_of(index):
        return pl.ds(pl.multiple_of(index * S, S), S)

    barrier = pltpu.get_barrier_semaphore()

    def greet(index):
        other = around(me, index, n)
        pl.semaphore_signal(
            barrier, inc=1, device_id=(other,), device_id_type=pl.DeviceIdType.MESH
        )

    each(n - 1, greet)
    fetched = [
        (points_in, points),
        (device_skeleton_in, device_skeleton),
        (charges_in, charges),
        (leaf_basis_in, leaf_basis),
        (device_basis_in, device_basis),
        (group_basis_in, group_own),
        (group_skeleton_in, group_skeleton),
        (cluster_basis_in, cluster_own),
        (cluster_skeleton_in, cluster_skeleton),
        (points_in, window.at[middle_slot, pl.ds(0, F)]),
        (charges_in, window.at[middle_slot, pl.ds(F, R)]),
    ]
    fetches = [
        pltpu.make_async_copy(here, there, local_sem.at[index])
        for index, (here, there) in enumerate(fetched)
    ]
    for index in (0, 1, 9, 10, 2, 3, 4, 5, 6, 7, 8):
        fetches[index].start()

    def lane_offset(index):
        return jnp.where(index < REACH // 2, index - REACH // 2, index - REACH // 2 + 1) * 2

    def lane_copy(index):
        offset = lane_offset(index)
        slot = middle_slot - offset
        return send(
            window.at[middle_slot],
            window.at[slot],
            window_send.at[index],
            window_recv.at[slot],
            jnp.clip(me + offset, 0, n - 1),
        )

    def inside(device):
        return (device >= 0) & (device < n)

    def start_lane(index):
        @pl.when(inside(me + lane_offset(index)))
        def _():
            lane_copy(index).start()

    def forward_copy(index):
        slot = index * 2
        landing = jnp.clip(slot - 1 + 2 * core, 0, 2 * REACH)
        return send(
            window.at[slot],
            window.at[landing],
            forward_send.at[index],
            window_recv.at[landing],
            sibling,
        )

    def forwarded(index):
        slot = index * 2
        landing = slot - 1 + 2 * core
        return inside(me + slot - middle_slot) & (landing >= 0) & (landing <= 2 * REACH)

    def arrived(slot):
        send(
            window.at[slot], window.at[slot], window_send.at[0], window_recv.at[slot], sibling
        ).wait_recv()

    fetches[0].wait()
    fetches[1].wait()
    device_points = jnp.zeros((F, S), jnp.float32)
    for inner in range(LEAVES_DEV):
        rows = slice(inner * leaf, (inner + 1) * leaf)
        device_points += pick(
            points[:, rows], one_hot_of(device_skeleton[...], leaf, inner * leaf)
        )
    device_nodes[child, 0:F, :] = device_points
    for index in range(2, len(fetches)):
        fetches[index].wait()
    pl.semaphore_wait(barrier, n - 1)
    for index in first_sends:
        start_lane(index)
    forward_copy(REACH // 2).start()

    def group_rows_copy(index):
        other = around(child, index, group)
        return send(
            group_own.at[:, columns_of(other)],
            group_rows.at[child],
            rows_send,
            rows_recv,
            group_first + other,
        )

    def cluster_rows_copy(index):
        other = around(place, index, cluster)
        return send(
            cluster_own.at[:, columns_of(other // group)],
            cluster_rows.at[place],
            cluster_rows_send,
            cluster_rows_recv,
            cluster_first + other,
        )

    device_weights = jnp.zeros((R, S), jnp.float32)
    for inner in range(LEAVES_DEV):
        rows = slice(inner * leaf, (inner + 1) * leaf)
        leaf_weights = product(charges[:, rows], leaf_basis[rows, :], 0)
        device_weights += product(
            leaf_weights, device_basis[inner * S : (inner + 1) * S, :], 0
        )
    device_nodes[child, F : F + R, :] = device_weights

    def device_copy(index):
        other = around(child, index, group)
        return send(
            device_nodes.at[child],
            device_nodes.at[child],
            device_send,
            device_recv,
            group_first + other,
        )


    each(group - 1, lambda index: device_copy(index).start())
    for index in second_sends:
        start_lane(index)
    each(group - 1, lambda index: group_rows_copy(index).start())
    each(cluster - 1, lambda index: cluster_rows_copy(index).start())
    group_rows[child] = group_own[:, columns_of(child)]
    cluster_rows[place] = cluster_own[:, columns_of(group_in_cluster)]
    all_of(device_nodes.at[pl.ds(0, group - 1)], device_send, device_recv).wait_recv()

    quarter_weights = jnp.zeros((R, quarter), jnp.float32)
    quarter_points = jnp.zeros((F, quarter), jnp.float32)
    for inner in range(group):
        quarter_weights += product(
            device_nodes[inner, F : F + R, :], group_own[:, inner * S : (inner + 1) * S], 1
        )
        quarter_points += pick(
            device_nodes[inner, 0:F, :], one_hot_of(group_skeleton[...], S, inner * S)
        )
    quarters[place] = jnp.concatenate([quarter_points, quarter_weights], axis=1)

    def quarter_copy(index):
        other = around(place, index, cluster)
        return send(
            quarters.at[place],
            quarters.at[place],
            quarter_send,
            quarter_recv,
            cluster_first + other,
        )


    each(cluster - 1, lambda index: quarter_copy(index).start())
    for index in third_sends:
        start_lane(index)
    all_of(quarters.at[pl.ds(0, cluster - 1)], quarter_send, quarter_recv).wait_recv()

    lane = lax.broadcasted_iota(jnp.int32, (F, 2 * quarter), 1)
    for pair in range(cluster // 2):
        even, odd = quarters[2 * pair], quarters[2 * pair + 1]
        columns = slice(pair * 2 * quarter, (pair + 1) * 2 * quarter)
        stack[0:F, columns] = jnp.where(lane < quarter, even, pltpu.roll(odd, quarter, 1))
        stack[F : F + R, columns] = jnp.where(lane < quarter, pltpu.roll(even, quarter, 1), odd)

    part_points = jnp.zeros((F, part), jnp.float32)
    for inner in range(group):
        part_points += pick(
            stack[0:F, inner * S : (inner + 1) * S],
            one_hot_of(cluster_skeleton[...], S, inner * S),
        )
    part_weights = product(stack[F : F + R, :], cluster_own[...], 1)
    node_rows = jnp.concatenate(
        [part_points, part_weights, jnp.zeros((128 - F - R, part), jnp.float32)], axis=0
    ).T
    parts[me] = node_rows[: part // 2] + pltpu.roll(node_rows[part // 2 :], F + R, 1)

    def part_copy(index):
        return send(
            parts.at[me],
            parts.at[me],
            part_send,
            part_recv,
            around(me, index, n),
        )


    each(n - 1, lambda index: part_copy(index).start())

    group_of = lax.broadcasted_iota(jnp.int32, (R, cluster * quarter), 1) // S
    side_weights = jnp.where(group_of != group_in_cluster, stack[F : F + R, :], 0.0)
    side = far_sum(side_weights, stack[0:F, columns_of(group_in_cluster)], stack[0:F, :])

    def hand_on(index):
        slot = index * 2

        @pl.when(inside(me + slot - middle_slot))
        def _():
            arrived(slot)

            @pl.when(forwarded(index))
            def _():
                forward_copy(index).start()

    for index in early_slots:
        if index != REACH // 2:
            hand_on(index)

    all_of(parts.at[pl.ds(0, n - 1)], part_send, part_recv).wait_recv()
    half = part // 2
    parts_turned[...] = parts[...].reshape(n * half, parts.shape[2]).T
    own_columns = pl.ds(pl.multiple_of((me // cluster) * cluster * half, cluster * half), cluster * half)
    cluster_of = lax.broadcasted_iota(jnp.int32, (R, n * half), 1) // (cluster * half)
    others = cluster_of != me // cluster
    upper = F + R
    all_points = jnp.concatenate(
        [parts_turned[0:F, :], parts_turned[upper : upper + F, :]], axis=1
    )
    all_weights = jnp.concatenate(
        [
            jnp.where(others, parts_turned[F:upper, :], 0.0),
            jnp.where(others, parts_turned[upper + F : upper + F + R, :], 0.0),
        ],
        axis=1,
    )
    own_points = jnp.concatenate(
        [parts_turned[0:F, own_columns], parts_turned[upper : upper + F, own_columns]], axis=1
    )
    top = far_sum(all_weights, own_points, all_points)

    for index in late_slots:
        hand_on(index)


    all_of(group_rows.at[pl.ds(0, group - 1)], rows_send, rows_recv).wait_recv()
    all_of(cluster_rows.at[pl.ds(0, cluster - 1)], cluster_rows_send, cluster_rows_recv).wait_recv()

    rows_of_cluster = jnp.concatenate(
        [
            cluster_rows[:, :half, :].reshape(cluster * half, S),
            cluster_rows[:, half:, :].reshape(cluster * half, S),
        ],
        axis=0,
    )
    down_group = side + product(top, rows_of_cluster, 0)
    down_device = product(down_group, group_rows[...].reshape(group * quarter, S), 0)
    for inner in range(LEAVES_DEV):
        rows = slice(inner * leaf, (inner + 1) * leaf)
        down_leaf = product(down_device, device_basis[inner * S : (inner + 1) * S, :], 1)
        far[:, rows] = product(down_leaf, leaf_basis[rows, :], 1)

    def landed(index):
        slot = index * 2 + 1

        @pl.when(inside(me + slot - middle_slot))
        def _():
            arrived(slot)

    each(REACH, landed)

    def lane_sent(index):
        @pl.when(inside(me + lane_offset(index)))
        def _():
            lane_copy(index).wait_send()

    def forward_sent(index):
        @pl.when(forwarded(index))
        def _():
            forward_copy(index).wait_send()

    each(REACH, lane_sent)
    each(REACH + 1, forward_sent)
    all_of(group_rows.at[pl.ds(0, group - 1)], rows_send, rows_recv).wait_send()
    all_of(cluster_rows.at[pl.ds(0, cluster - 1)], cluster_rows_send, cluster_rows_recv).wait_send()
    all_of(device_nodes.at[pl.ds(0, group - 1)], device_send, device_recv).wait_send()
    all_of(quarters.at[pl.ds(0, cluster - 1)], quarter_send, quarter_recv).wait_send()
    all_of(parts.at[pl.ds(0, n - 1)], part_send, part_recv).wait_send()


def tree(points, charges, leaf_basis, device_basis, device_skeleton, group_basis, group_skeleton,
         cluster_basis, cluster_skeleton):
    n = lax.axis_size("leaf")
    quarter, part = group_basis.shape[1], cluster_basis.shape[1]
    group, cluster = S // quarter, S // part
    width = points.shape[1]
    vmem = pl.BlockSpec(memory_space=pltpu.VMEM)
    dma = pltpu.SemaphoreType.DMA
    return pl.pallas_call(
        functools.partial(tree_kernel, n),
        out_shape=(
            jax.ShapeDtypeStruct((2 * REACH + 1, F + R, width), jnp.float32),
            jax.ShapeDtypeStruct((R, width), jnp.float32),
        ),
        in_specs=[pl.BlockSpec(memory_space=pl.ANY)] * 9,
        out_specs=(pl.BlockSpec(memory_space=pl.ANY), vmem),
        scratch_shapes=[
            pltpu.VMEM(points.shape, jnp.float32),
            pltpu.VMEM(charges.shape, jnp.float32),
            pltpu.VMEM(leaf_basis.shape, jnp.float32),
            pltpu.VMEM(device_basis.shape, jnp.float32),
            pltpu.VMEM(device_skeleton.shape, jnp.int32),
            pltpu.VMEM((quarter, group * S), jnp.float32),
            pltpu.VMEM((1, quarter), jnp.int32),
            pltpu.VMEM((part, group * S), jnp.float32),
            pltpu.VMEM((1, part), jnp.int32),
            pltpu.VMEM((group, quarter, S), jnp.float32),
            pltpu.VMEM((cluster, part, S), jnp.float32),
            pltpu.VMEM((group, F + R, S), jnp.float32),
            pltpu.VMEM((cluster, F, 2 * quarter), jnp.float32),
            pltpu.VMEM((F + R, cluster * quarter), jnp.float32),
            pltpu.VMEM((n, part // 2, 128), jnp.float32),
            pltpu.VMEM((128, n * part // 2), jnp.float32),
            dma((11,)),
            dma((REACH,)),
            dma((REACH + 1,)),
            dma((2 * REACH + 1,)),
            dma(()),
            dma(()),
            dma(()),
            dma(()),
            dma(()),
            dma(()),
            dma(()),
            dma(()),
            dma(()),
            dma(()),
        ],
        compiler_params=pltpu.CompilerParams(
            collective_id=0, has_side_effects=True, vmem_limit_bytes=VMEM_BYTES
        ),
        name="tree_and_window",
    )(
        points,
        charges,
        leaf_basis,
        device_basis,
        device_skeleton,
        group_basis.T,
        group_skeleton[None, :],
        cluster_basis.T,
        cluster_skeleton[None, :],
    )


def shards(points, charges, near_list, near_count, leaf_basis, device_basis, device_skeleton,
           group_basis, group_skeleton, cluster_basis, cluster_skeleton):
    window, far = tree(points, charges, leaf_basis, device_basis, device_skeleton, group_basis,
                       group_skeleton, cluster_basis, cluster_skeleton)
    return near_field(window, near_list, near_count, far)


def solution(mesh):
    return jax.shard_map(
        shards,
        mesh=mesh,
        in_specs=(
            P(None, "leaf"),
            P(None, "leaf"),
            P("leaf", None),
            P("leaf"),
            P("leaf", None),
            P("leaf", None),
            P("leaf", None),
            P(None, "leaf"),
            P("leaf"),
            P(None, "leaf"),
            P("leaf"),
        ),
        out_specs=P(None, "leaf"),
        check_vma=False,
    )
```

```python
import functools

import jax
import jax.numpy as jnp
from jax import lax
from jax.experimental import pallas as pl
from jax.experimental.pallas import tpu as pltpu
from jax.sharding import PartitionSpec as P

F = 16
R = 16
S = 256
REACH = 8
LEAVES_DEV = 4
VMEM_BYTES = 60 * 1024 * 1024


inverse_spread = 1.0 / 16.0


def split3(value):
    high = value.astype(jnp.bfloat16)
    rest = value - high.astype(jnp.float32)
    middle = rest.astype(jnp.bfloat16)
    low = (rest - middle.astype(jnp.float32)).astype(jnp.bfloat16)
    return high, middle, low


def norm_rows(squares, first):
    high, middle, low = (piece.astype(jnp.float32) for piece in split3(squares))
    row = lax.broadcasted_iota(jnp.int32, (16, squares.shape[1]), 0)
    ones = 3 - first
    block = jnp.where((row >= ones) & (row < ones + 3), 1.0, 0.0)
    block = jnp.where(row == first, high, block)
    block = jnp.where(row == first + 1, middle, block)
    return jnp.where(row == first + 2, low, block)


def split2(value):
    high = value.astype(jnp.bfloat16)
    return high, (value - high.astype(jnp.float32)).astype(jnp.bfloat16)


def product(left, right, contract):
    dims = (((1,), (contract,)), ((), ()))
    left_high, left_low = split2(left)
    right_high, right_low = split2(right)
    rows = left.shape[0]
    both = lax.dot_general(
        jnp.concatenate([left_high, left_low], axis=0),
        right_high,
        dims,
        preferred_element_type=jnp.float32,
    )
    rest = lax.dot_general(left_high, right_low, dims, preferred_element_type=jnp.float32)
    return both[:rows] + (both[rows:] + rest)


def pick(values, one_hot):
    stacked = jnp.concatenate(list(split3(values)), axis=0)
    picked = jnp.dot(stacked, one_hot, preferred_element_type=jnp.float32)
    rows = values.shape[0]
    return picked[:rows] + picked[rows : 2 * rows] + picked[2 * rows :]


def source_rows(block):
    scale = inverse_spread
    high, middle, low = split3(block)
    squares = jnp.sum(block * block, axis=0, keepdims=True) * (-scale)
    norms = norm_rows(squares, 3).astype(jnp.bfloat16)
    return (high, middle, high, low, high, middle, norms, jnp.zeros_like(norms))


def target_rows(block):
    scale = inverse_spread
    high, middle, low = (p.astype(jnp.float32) for p in split3(block * (2.0 * scale)))
    squares = jnp.sum(block * block, axis=0, keepdims=True) * (-scale)
    norms = norm_rows(squares, 0)
    stacked = jnp.concatenate(
        [high, high, middle, high, low, middle, norms, jnp.zeros_like(norms)], axis=0
    )
    return stacked.T.astype(jnp.bfloat16)


def far_sum(weights, targets, sources):
    power = jnp.dot(
        target_rows(targets),
        jnp.concatenate(list(source_rows(sources)), axis=0),
        preferred_element_type=jnp.float32,
    )
    return product(weights, jnp.exp(power), 1)


def one_hot_of(indices, rows, first):
    row = lax.broadcasted_iota(jnp.int32, (rows, indices.shape[1]), 0) + first
    return (row == indices).astype(jnp.float32).astype(jnp.bfloat16)


def near_kernel(
    list_ref,
    count_ref,
    window_ref,
    far_ref,
    out_ref,
    window,
    source,
    charge,
    target,
    power,
    tile,
    total,
    plan_leaf,
    plan_source,
    sems,
):
    devices, _, width = window.shape
    leaf = source.shape[2]
    leaves_dev = width // leaf
    first_leaf = (lax.axis_index("leaf") - REACH) * leaves_dev

    def block_copy(device):
        return pltpu.make_async_copy(window_ref.at[device], window.at[device], sems.at[device])

    def fetch(device, carry):
        block_copy(device).start()
        return carry

    lax.fori_loop(0, devices, fetch, 0)

    def prepare(device, carry):
        block_copy(device).wait()
        for inner in range(leaves_dev):
            columns = slice(inner * leaf, (inner + 1) * leaf)
            slot = device * leaves_dev + inner
            for place, piece in enumerate(source_rows(window[device, 0:F, columns])):
                source[slot, place * 16 : (place + 1) * 16, :] = piece
            charge[slot] = window[device, F : F + R, columns].astype(jnp.bfloat16)
        return carry

    lax.fori_loop(0, devices, prepare, 0)

    end = jnp.int32(0)
    for inner in range(leaves_dev):
        columns = slice(inner * leaf, (inner + 1) * leaf)
        target[inner] = target_rows(window[REACH, 0:F, columns])
        total[inner] = jnp.zeros(total.shape[1:], jnp.float32)

        def enter(slot, place, inner=inner):
            plan_leaf[place] = inner
            plan_source[place] = list_ref[inner, slot] - first_leaf
            return place + 1

        end = lax.fori_loop(0, count_ref[inner], enter, end)
    power[...] = jnp.zeros_like(power)
    tile[...] = jnp.zeros_like(tile)

    def step(index, carry):
        done = jnp.clip(index - 2, 0, end - 1)
        live = (index >= 2).astype(jnp.float32)
        weights = (charge[plan_source[done]].astype(jnp.float32) * live).astype(jnp.bfloat16)
        total[plan_leaf[done]] += lax.dot_general(
            weights, tile[...], (((1,), (1,)), ((), ())), preferred_element_type=jnp.float32
        )
        tile[...] = jnp.exp(power[...]).astype(jnp.bfloat16)
        fresh = jnp.minimum(index, end - 1)
        power[...] = jnp.dot(
            target[plan_leaf[fresh]], source[plan_source[fresh]], preferred_element_type=jnp.float32
        )
        return carry

    lax.fori_loop(0, end + 2, step, 0)
    for inner in range(leaves_dev):
        columns = slice(inner * leaf, (inner + 1) * leaf)
        out_ref[:, columns] = total[inner] + far_ref[:, columns]


def near_field(window, near_list, near_count, far):
    devices, rows, width = window.shape
    leaves_dev = near_list.shape[0]
    leaf = width // leaves_dev
    slots = devices * leaves_dev
    vmem = pl.BlockSpec(memory_space=pltpu.VMEM)
    smem = pl.BlockSpec(memory_space=pltpu.SMEM)
    return pl.pallas_call(
        near_kernel,
        out_shape=jax.ShapeDtypeStruct((R, width), jnp.float32),
        in_specs=[smem, smem, pl.BlockSpec(memory_space=pl.ANY), vmem],
        out_specs=vmem,
        scratch_shapes=[
            pltpu.VMEM((devices, rows, width), jnp.float32),
            pltpu.VMEM((slots, 128, leaf), jnp.bfloat16),
            pltpu.VMEM((slots, R, leaf), jnp.bfloat16),
            pltpu.VMEM((leaves_dev, leaf, 128), jnp.bfloat16),
            pltpu.VMEM((leaf, leaf), jnp.float32),
            pltpu.VMEM((leaf, leaf), jnp.bfloat16),
            pltpu.VMEM((leaves_dev, R, leaf), jnp.float32),
            pltpu.SMEM((near_list.size,), jnp.int32),
            pltpu.SMEM((near_list.size,), jnp.int32),
            pltpu.SemaphoreType.DMA((devices,)),
        ],
        compiler_params=pltpu.CompilerParams(vmem_limit_bytes=VMEM_BYTES),
        name="near_tiles",
    )(near_list, near_count, window, far)


def tree_kernel(
    n,
    points_in,
    charges_in,
    leaf_basis_in,
    device_basis_in,
    device_skeleton_in,
    group_basis_in,
    group_skeleton_in,
    cluster_basis_in,
    cluster_skeleton_in,
    window,
    far,
    points,
    charges,
    leaf_basis,
    device_basis,
    device_skeleton,
    group_own,
    group_skeleton,
    cluster_own,
    cluster_skeleton,
    group_rows,
    cluster_rows,
    device_nodes,
    quarters,
    stack,
    parts,
    parts_turned,
    local_sem,
    window_send,
    forward_send,
    window_recv,
    rows_send,
    rows_recv,
    cluster_rows_send,
    cluster_rows_recv,
    device_send,
    device_recv,
    quarter_send,
    quarter_recv,
    part_send,
    part_recv,
):
    me = lax.axis_index("leaf")
    group = device_nodes.shape[0]
    cluster = quarters.shape[0]
    quarter = group_own.shape[0]
    part = cluster_own.shape[0]
    leaf = points.shape[1] // LEAVES_DEV
    place, child = me % cluster, me % group
    group_first, cluster_first = me - child, me - place
    group_in_cluster = place // group
    core = me % 2
    sibling = me + 1 - 2 * core
    middle_slot = REACH
    last = REACH - 1
    first_sends = (0, last)
    second_sends = tuple(range(REACH // 4, REACH - REACH // 4))
    third_sends = tuple(i for i in range(1, last) if i not in second_sends)
    late_slots = tuple(i if i < REACH // 2 else i + 1 for i in third_sends)
    early_slots = tuple(i for i in range(REACH + 1) if i not in late_slots)

    def send(source, destination, send_sem, recv_sem, device):
        return pltpu.make_async_remote_copy(
            src_ref=source,
            dst_ref=destination,
            send_sem=send_sem,
            recv_sem=recv_sem,
            device_id=(device,),
            device_id_type=pl.DeviceIdType.MESH,
        )

    def around(position, index, size):
        other = position + 1 + index
        return jnp.where(other >= size, other - size, other)

    def all_of(ref, send_sem, recv_sem):
        return send(ref, ref, send_sem, recv_sem, sibling)

    def each(count, body):
        def step(index, carry):
            body(index)
            return carry

        lax.fori_loop(0, count, step, 0)

    def columns_of(index):
        return pl.ds(pl.multiple_of(index * S, S), S)

    barrier = pltpu.get_barrier_semaphore()

    def greet(index):
        other = around(me, index, n)
        pl.semaphore_signal(
            barrier, inc=1, device_id=(other,), device_id_type=pl.DeviceIdType.MESH
        )

    each(n - 1, greet)
    fetched = [
        (points_in, points),
        (device_skeleton_in, device_skeleton),
        (charges_in, charges),
        (leaf_basis_in, leaf_basis),
        (device_basis_in, device_basis),
        (group_basis_in, group_own),
        (group_skeleton_in, group_skeleton),
        (cluster_basis_in, cluster_own),
        (cluster_skeleton_in, cluster_skeleton),
        (points_in, window.at[middle_slot, pl.ds(0, F)]),
        (charges_in, window.at[middle_slot, pl.ds(F, R)]),
    ]
    fetches = [
        pltpu.make_async_copy(here, there, local_sem.at[index])
        for index, (here, there) in enumerate(fetched)
    ]
    for index in (0, 1, 9, 10, 2, 3, 4, 5, 6, 7, 8):
        fetches[index].start()

    def lane_offset(index):
        return jnp.where(index < REACH // 2, index - REACH // 2, index - REACH // 2 + 1) * 2

    def lane_copy(index):
        offset = lane_offset(index)
        slot = middle_slot - offset
        return send(
            window.at[middle_slot],
            window.at[slot],
            window_send.at[index],
            window_recv.at[slot],
            jnp.clip(me + offset, 0, n - 1),
        )

    def inside(device):
        return (device >= 0) & (device < n)

    def start_lane(index):
        @pl.when(inside(me + lane_offset(index)))
        def _():
            lane_copy(index).start()

    def forward_copy(index):
        slot = index * 2
        landing = jnp.clip(slot - 1 + 2 * core, 0, 2 * REACH)
        return send(
            window.at[slot],
            window.at[landing],
            forward_send.at[index],
            window_recv.at[landing],
            sibling,
        )

    def forwarded(index):
        slot = index * 2
        landing = slot - 1 + 2 * core
        return inside(me + slot - middle_slot) & (landing >= 0) & (landing <= 2 * REACH)

    def arrived(slot):
        send(
            window.at[slot], window.at[slot], window_send.at[0], window_recv.at[slot], sibling
        ).wait_recv()

    fetches[0].wait()
    fetches[1].wait()
    device_points = jnp.zeros((F, S), jnp.float32)
    for inner in range(LEAVES_DEV):
        rows = slice(inner * leaf, (inner + 1) * leaf)
        device_points += pick(
            points[:, rows], one_hot_of(device_skeleton[...], leaf, inner * leaf)
        )
    device_nodes[child, 0:F, :] = device_points
    for index in range(2, len(fetches)):
        fetches[index].wait()
    pl.semaphore_wait(barrier, n - 1)
    for index in first_sends:
        start_lane(index)
    forward_copy(REACH // 2).start()

    def group_rows_copy(index):
        other = around(child, index, group)
        return send(
            group_own.at[:, columns_of(other)],
            group_rows.at[child],
            rows_send,
            rows_recv,
            group_first + other,
        )

    def cluster_rows_copy(index):
        other = around(place, index, cluster)
        return send(
            cluster_own.at[:, columns_of(other // group)],
            cluster_rows.at[place],
            cluster_rows_send,
            cluster_rows_recv,
            cluster_first + other,
        )

    device_weights = jnp.zeros((R, S), jnp.float32)
    for inner in range(LEAVES_DEV):
        rows = slice(inner * leaf, (inner + 1) * leaf)
        leaf_weights = product(charges[:, rows], leaf_basis[rows, :], 0)
        device_weights += product(
            leaf_weights, device_basis[inner * S : (inner + 1) * S, :], 0
        )
    device_nodes[child, F : F + R, :] = device_weights

    def device_copy(index):
        other = around(child, index, group)
        return send(
            device_nodes.at[child],
            device_nodes.at[child],
            device_send,
            device_recv,
            group_first + other,
        )


    each(group - 1, lambda index: device_copy(index).start())
    each(group - 1, lambda index: group_rows_copy(index).start())
    each(cluster - 1, lambda index: cluster_rows_copy(index).start())
    group_rows[child] = group_own[:, columns_of(child)]
    cluster_rows[place] = cluster_own[:, columns_of(group_in_cluster)]
    all_of(device_nodes.at[pl.ds(0, group - 1)], device_send, device_recv).wait_recv()

    quarter_weights = jnp.zeros((R, quarter), jnp.float32)
    quarter_points = jnp.zeros((F, quarter), jnp.float32)
    for inner in range(group):
        quarter_weights += product(
            device_nodes[inner, F : F + R, :], group_own[:, inner * S : (inner + 1) * S], 1
        )
        quarter_points += pick(
            device_nodes[inner, 0:F, :], one_hot_of(group_skeleton[...], S, inner * S)
        )
    quarters[place] = jnp.concatenate([quarter_points, quarter_weights], axis=1)

    def quarter_copy(index):
        other = around(place, index, cluster)
        return send(
            quarters.at[place],
            quarters.at[place],
            quarter_send,
            quarter_recv,
            cluster_first + other,
        )


    each(cluster - 1, lambda index: quarter_copy(index).start())
    for index in second_sends:
        start_lane(index)
    all_of(quarters.at[pl.ds(0, cluster - 1)], quarter_send, quarter_recv).wait_recv()

    lane = lax.broadcasted_iota(jnp.int32, (F, 2 * quarter), 1)
    for pair in range(cluster // 2):
        even, odd = quarters[2 * pair], quarters[2 * pair + 1]
        columns = slice(pair * 2 * quarter, (pair + 1) * 2 * quarter)
        stack[0:F, columns] = jnp.where(lane < quarter, even, pltpu.roll(odd, quarter, 1))
        stack[F : F + R, columns] = jnp.where(lane < quarter, pltpu.roll(even, quarter, 1), odd)

    part_points = jnp.zeros((F, part), jnp.float32)
    for inner in range(group):
        part_points += pick(
            stack[0:F, inner * S : (inner + 1) * S],
            one_hot_of(cluster_skeleton[...], S, inner * S),
        )
    part_weights = product(stack[F : F + R, :], cluster_own[...], 1)
    node_rows = jnp.concatenate(
        [part_points, part_weights, jnp.zeros((128 - F - R, part), jnp.float32)], axis=0
    ).T
    parts[me] = node_rows[: part // 2] + pltpu.roll(node_rows[part // 2 :], F + R, 1)

    def part_copy(index):
        return send(
            parts.at[me],
            parts.at[me],
            part_send,
            part_recv,
            around(me, index, n),
        )


    each(n - 1, lambda index: part_copy(index).start())
    for index in third_sends:
        start_lane(index)

    group_of = lax.broadcasted_iota(jnp.int32, (R, cluster * quarter), 1) // S
    side_weights = jnp.where(group_of != group_in_cluster, stack[F : F + R, :], 0.0)
    side = far_sum(side_weights, stack[0:F, columns_of(group_in_cluster)], stack[0:F, :])

    def hand_on(index):
        slot = index * 2

        @pl.when(inside(me + slot - middle_slot))
        def _():
            arrived(slot)

            @pl.when(forwarded(index))
            def _():
                forward_copy(index).start()

    for index in early_slots:
        if index != REACH // 2:
            hand_on(index)

    all_of(parts.at[pl.ds(0, n - 1)], part_send, part_recv).wait_recv()
    half = part // 2
    parts_turned[...] = parts[...].reshape(n * half, parts.shape[2]).T
    own_columns = pl.ds(pl.multiple_of((me // cluster) * cluster * half, cluster * half), cluster * half)
    cluster_of = lax.broadcasted_iota(jnp.int32, (R, n * half), 1) // (cluster * half)
    others = cluster_of != me // cluster
    upper = F + R
    all_points = jnp.concatenate(
        [parts_turned[0:F, :], parts_turned[upper : upper + F, :]], axis=1
    )
    all_weights = jnp.concatenate(
        [
            jnp.where(others, parts_turned[F:upper, :], 0.0),
            jnp.where(others, parts_turned[upper + F : upper + F + R, :], 0.0),
        ],
        axis=1,
    )
    own_points = jnp.concatenate(
        [parts_turned[0:F, own_columns], parts_turned[upper : upper + F, own_columns]], axis=1
    )
    top = far_sum(all_weights, own_points, all_points)


    all_of(group_rows.at[pl.ds(0, group - 1)], rows_send, rows_recv).wait_recv()
    all_of(cluster_rows.at[pl.ds(0, cluster - 1)], cluster_rows_send, cluster_rows_recv).wait_recv()

    rows_of_cluster = jnp.concatenate(
        [
            cluster_rows[:, :half, :].reshape(cluster * half, S),
            cluster_rows[:, half:, :].reshape(cluster * half, S),
        ],
        axis=0,
    )
    down_group = side + product(top, rows_of_cluster, 0)
    down_device = product(down_group, group_rows[...].reshape(group * quarter, S), 0)
    for index in late_slots:
        hand_on(index)
    for inner in range(LEAVES_DEV):
        rows = slice(inner * leaf, (inner + 1) * leaf)
        down_leaf = product(down_device, device_basis[inner * S : (inner + 1) * S, :], 1)
        far[:, rows] = product(down_leaf, leaf_basis[rows, :], 1)

    def landed(index):
        slot = index * 2 + 1

        @pl.when(inside(me + slot - middle_slot))
        def _():
            arrived(slot)

    each(REACH, landed)

    def lane_sent(index):
        @pl.when(inside(me + lane_offset(index)))
        def _():
            lane_copy(index).wait_send()

    def forward_sent(index):
        @pl.when(forwarded(index))
        def _():
            forward_copy(index).wait_send()

    each(REACH, lane_sent)
    each(REACH + 1, forward_sent)
    all_of(group_rows.at[pl.ds(0, group - 1)], rows_send, rows_recv).wait_send()
    all_of(cluster_rows.at[pl.ds(0, cluster - 1)], cluster_rows_send, cluster_rows_recv).wait_send()
    all_of(device_nodes.at[pl.ds(0, group - 1)], device_send, device_recv).wait_send()
    all_of(quarters.at[pl.ds(0, cluster - 1)], quarter_send, quarter_recv).wait_send()
    all_of(parts.at[pl.ds(0, n - 1)], part_send, part_recv).wait_send()


def tree(points, charges, leaf_basis, device_basis, device_skeleton, group_basis, group_skeleton,
         cluster_basis, cluster_skeleton):
    n = lax.axis_size("leaf")
    quarter, part = group_basis.shape[1], cluster_basis.shape[1]
    group, cluster = S // quarter, S // part
    width = points.shape[1]
    vmem = pl.BlockSpec(memory_space=pltpu.VMEM)
    dma = pltpu.SemaphoreType.DMA
    return pl.pallas_call(
        functools.partial(tree_kernel, n),
        out_shape=(
            jax.ShapeDtypeStruct((2 * REACH + 1, F + R, width), jnp.float32),
            jax.ShapeDtypeStruct((R, width), jnp.float32),
        ),
        in_specs=[pl.BlockSpec(memory_space=pl.ANY)] * 9,
        out_specs=(pl.BlockSpec(memory_space=pl.ANY), vmem),
        scratch_shapes=[
            pltpu.VMEM(points.shape, jnp.float32),
            pltpu.VMEM(charges.shape, jnp.float32),
            pltpu.VMEM(leaf_basis.shape, jnp.float32),
            pltpu.VMEM(device_basis.shape, jnp.float32),
            pltpu.VMEM(device_skeleton.shape, jnp.int32),
            pltpu.VMEM((quarter, group * S), jnp.float32),
            pltpu.VMEM((1, quarter), jnp.int32),
            pltpu.VMEM((part, group * S), jnp.float32),
            pltpu.VMEM((1, part), jnp.int32),
            pltpu.VMEM((group, quarter, S), jnp.float32),
            pltpu.VMEM((cluster, part, S), jnp.float32),
            pltpu.VMEM((group, F + R, S), jnp.float32),
            pltpu.VMEM((cluster, F, 2 * quarter), jnp.float32),
            pltpu.VMEM((F + R, cluster * quarter), jnp.float32),
            pltpu.VMEM((n, part // 2, 128), jnp.float32),
            pltpu.VMEM((128, n * part // 2), jnp.float32),
            dma((11,)),
            dma((REACH,)),
            dma((REACH + 1,)),
            dma((2 * REACH + 1,)),
            dma(()),
            dma(()),
            dma(()),
            dma(()),
            dma(()),
            dma(()),
            dma(()),
            dma(()),
            dma(()),
            dma(()),
        ],
        compiler_params=pltpu.CompilerParams(
            collective_id=0, has_side_effects=True, vmem_limit_bytes=VMEM_BYTES
        ),
        name="tree_and_window",
    )(
        points,
        charges,
        leaf_basis,
        device_basis,
        device_skeleton,
        group_basis.T,
        group_skeleton[None, :],
        cluster_basis.T,
        cluster_skeleton[None, :],
    )


def shards(points, charges, near_list, near_count, leaf_basis, device_basis, device_skeleton,
           group_basis, group_skeleton, cluster_basis, cluster_skeleton):
    window, far = tree(points, charges, leaf_basis, device_basis, device_skeleton, group_basis,
                       group_skeleton, cluster_basis, cluster_skeleton)
    return near_field(window, near_list, near_count, far)


def solution(mesh):
    return jax.shard_map(
        shards,
        mesh=mesh,
        in_specs=(
            P(None, "leaf"),
            P(None, "leaf"),
            P("leaf", None),
            P("leaf"),
            P("leaf", None),
            P("leaf", None),
            P("leaf", None),
            P(None, "leaf"),
            P("leaf"),
            P(None, "leaf"),
            P("leaf"),
        ),
        out_specs=P(None, "leaf"),
        check_vma=False,
    )
```

```python
import functools
import math

import jax
import jax.numpy as jnp
from jax import lax
from jax.experimental import pallas as pl
from jax.experimental.pallas import tpu as pltpu
from jax.sharding import PartitionSpec as P

F = 16
R = 16
S = 256
REACH = 8
LEAVES_DEV = 4
VMEM_BYTES = 60 * 1024 * 1024


inverse_spread = 1.0 / 16.0


def split3(value):
    high = value.astype(jnp.bfloat16)
    rest = value - high.astype(jnp.float32)
    middle = rest.astype(jnp.bfloat16)
    low = (rest - middle.astype(jnp.float32)).astype(jnp.bfloat16)
    return high, middle, low


def norm_rows(squares, first):
    high, middle, low = (piece.astype(jnp.float32) for piece in split3(squares))
    row = lax.broadcasted_iota(jnp.int32, (16, squares.shape[1]), 0)
    ones = 3 - first
    block = jnp.where((row >= ones) & (row < ones + 3), 1.0, 0.0)
    block = jnp.where(row == first, high, block)
    block = jnp.where(row == first + 1, middle, block)
    return jnp.where(row == first + 2, low, block)


def split2(value):
    high = value.astype(jnp.bfloat16)
    return high, (value - high.astype(jnp.float32)).astype(jnp.bfloat16)


def product(left, right, contract):
    dims = (((1,), (contract,)), ((), ()))
    left_high, left_low = split2(left)
    right_high, right_low = split2(right)
    rows = left.shape[0]
    both = lax.dot_general(
        jnp.concatenate([left_high, left_low], axis=0),
        right_high,
        dims,
        preferred_element_type=jnp.float32,
    )
    rest = lax.dot_general(left_high, right_low, dims, preferred_element_type=jnp.float32)
    return both[:rows] + (both[rows:] + rest)


def pick(values, one_hot):
    stacked = jnp.concatenate(list(split3(values)), axis=0)
    picked = jnp.dot(stacked, one_hot, preferred_element_type=jnp.float32)
    rows = values.shape[0]
    return picked[:rows] + picked[rows : 2 * rows] + picked[2 * rows :]


def source_rows(block):
    scale = inverse_spread * math.log2(math.e)
    high, middle, low = split3(block)
    squares = jnp.sum(block * block, axis=0, keepdims=True) * (-scale)
    norms = norm_rows(squares, 3).astype(jnp.bfloat16)
    return (high, middle, high, low, high, middle, norms, jnp.zeros_like(norms))


def target_rows(block):
    scale = inverse_spread * math.log2(math.e)
    high, middle, low = (p.astype(jnp.float32) for p in split3(block * (2.0 * scale)))
    squares = jnp.sum(block * block, axis=0, keepdims=True) * (-scale)
    norms = norm_rows(squares, 0)
    stacked = jnp.concatenate(
        [high, high, middle, high, low, middle, norms, jnp.zeros_like(norms)], axis=0
    )
    return stacked.T.astype(jnp.bfloat16)


def far_sum(weights, targets, sources):
    power = jnp.dot(
        target_rows(targets),
        jnp.concatenate(list(source_rows(sources)), axis=0),
        preferred_element_type=jnp.float32,
    )
    return product(weights, jnp.exp2(power), 1)


def one_hot_of(indices, rows, first):
    row = lax.broadcasted_iota(jnp.int32, (rows, indices.shape[1]), 0) + first
    return (row == indices).astype(jnp.float32).astype(jnp.bfloat16)


def near_kernel(
    list_ref,
    count_ref,
    window_ref,
    far_ref,
    out_ref,
    window,
    source,
    charge,
    target,
    power,
    tile,
    total,
    plan_leaf,
    plan_source,
    sems,
):
    devices, _, width = window.shape
    leaf = source.shape[2]
    leaves_dev = width // leaf
    first_leaf = (lax.axis_index("leaf") - REACH) * leaves_dev

    def block_copy(device):
        return pltpu.make_async_copy(window_ref.at[device], window.at[device], sems.at[device])

    def fetch(device, carry):
        block_copy(device).start()
        return carry

    lax.fori_loop(0, devices, fetch, 0)

    def prepare(device, carry):
        block_copy(device).wait()
        for inner in range(leaves_dev):
            columns = slice(inner * leaf, (inner + 1) * leaf)
            slot = device * leaves_dev + inner
            for place, piece in enumerate(source_rows(window[device, 0:F, columns])):
                source[slot, place * 16 : (place + 1) * 16, :] = piece
            charge[slot] = window[device, F : F + R, columns].astype(jnp.bfloat16)
        return carry

    lax.fori_loop(0, devices, prepare, 0)

    end = jnp.int32(0)
    for inner in range(leaves_dev):
        columns = slice(inner * leaf, (inner + 1) * leaf)
        target[inner] = target_rows(window[REACH, 0:F, columns])
        total[inner] = jnp.zeros(total.shape[1:], jnp.float32)

        def enter(slot, place, inner=inner):
            plan_leaf[place] = inner
            plan_source[place] = list_ref[inner, slot] - first_leaf
            return place + 1

        end = lax.fori_loop(0, count_ref[inner], enter, end)
    power[...] = jnp.zeros_like(power)
    tile[...] = jnp.zeros_like(tile)

    def step(index, carry):
        done = jnp.clip(index - 2, 0, end - 1)
        live = (index >= 2).astype(jnp.float32)
        weights = (charge[plan_source[done]].astype(jnp.float32) * live).astype(jnp.bfloat16)
        total[plan_leaf[done]] += lax.dot_general(
            weights, tile[...], (((1,), (1,)), ((), ())), preferred_element_type=jnp.float32
        )
        tile[...] = jnp.exp2(power[...]).astype(jnp.bfloat16)
        fresh = jnp.minimum(index, end - 1)
        power[...] = jnp.dot(
            target[plan_leaf[fresh]], source[plan_source[fresh]], preferred_element_type=jnp.float32
        )
        return carry

    lax.fori_loop(0, end + 2, step, 0)
    for inner in range(leaves_dev):
        columns = slice(inner * leaf, (inner + 1) * leaf)
        out_ref[:, columns] = total[inner] + far_ref[:, columns]


def near_field(window, near_list, near_count, far):
    devices, rows, width = window.shape
    leaves_dev = near_list.shape[0]
    leaf = width // leaves_dev
    slots = devices * leaves_dev
    vmem = pl.BlockSpec(memory_space=pltpu.VMEM)
    smem = pl.BlockSpec(memory_space=pltpu.SMEM)
    return pl.pallas_call(
        near_kernel,
        out_shape=jax.ShapeDtypeStruct((R, width), jnp.float32),
        in_specs=[smem, smem, pl.BlockSpec(memory_space=pl.ANY), vmem],
        out_specs=vmem,
        scratch_shapes=[
            pltpu.VMEM((devices, rows, width), jnp.float32),
            pltpu.VMEM((slots, 128, leaf), jnp.bfloat16),
            pltpu.VMEM((slots, R, leaf), jnp.bfloat16),
            pltpu.VMEM((leaves_dev, leaf, 128), jnp.bfloat16),
            pltpu.VMEM((leaf, leaf), jnp.float32),
            pltpu.VMEM((leaf, leaf), jnp.bfloat16),
            pltpu.VMEM((leaves_dev, R, leaf), jnp.float32),
            pltpu.SMEM((near_list.size,), jnp.int32),
            pltpu.SMEM((near_list.size,), jnp.int32),
            pltpu.SemaphoreType.DMA((devices,)),
        ],
        compiler_params=pltpu.CompilerParams(vmem_limit_bytes=VMEM_BYTES),
        name="near_tiles",
    )(near_list, near_count, window, far)


def tree_kernel(
    n,
    points_in,
    charges_in,
    leaf_basis_in,
    device_basis_in,
    device_skeleton_in,
    group_basis_in,
    group_skeleton_in,
    cluster_basis_in,
    cluster_skeleton_in,
    window,
    far,
    points,
    charges,
    leaf_basis,
    device_basis,
    device_skeleton,
    group_own,
    group_skeleton,
    cluster_own,
    cluster_skeleton,
    group_rows,
    cluster_rows,
    device_nodes,
    quarters,
    stack,
    parts,
    parts_turned,
    local_sem,
    window_send,
    forward_send,
    window_recv,
    rows_send,
    rows_recv,
    cluster_rows_send,
    cluster_rows_recv,
    device_send,
    device_recv,
    quarter_send,
    quarter_recv,
    part_send,
    part_recv,
):
    me = lax.axis_index("leaf")
    group = device_nodes.shape[0]
    cluster = quarters.shape[0]
    quarter = group_own.shape[0]
    part = cluster_own.shape[0]
    leaf = points.shape[1] // LEAVES_DEV
    place, child = me % cluster, me % group
    group_first, cluster_first = me - child, me - place
    group_in_cluster = place // group
    core = me % 2
    sibling = me + 1 - 2 * core
    middle_slot = REACH
    last = REACH - 1
    first_sends = (0, last)
    second_sends = (REACH // 2 - 1, REACH // 2)
    third_sends = tuple(range(REACH // 4, REACH // 2 - 1)) + tuple(
        range(REACH // 2 + 1, REACH - REACH // 4)
    )
    fourth_sends = tuple(
        i for i in range(1, last) if i not in second_sends and i not in third_sends
    )
    late_slots = tuple(i if i < REACH // 2 else i + 1 for i in fourth_sends)
    early_slots = tuple(i for i in range(REACH + 1) if i not in late_slots)

    def send(source, destination, send_sem, recv_sem, device):
        return pltpu.make_async_remote_copy(
            src_ref=source,
            dst_ref=destination,
            send_sem=send_sem,
            recv_sem=recv_sem,
            device_id=(device,),
            device_id_type=pl.DeviceIdType.MESH,
        )

    def around(position, index, size):
        other = position + 1 + index
        return jnp.where(other >= size, other - size, other)

    def all_of(ref, send_sem, recv_sem):
        return send(ref, ref, send_sem, recv_sem, sibling)

    def each(count, body):
        def step(index, carry):
            body(index)
            return carry

        lax.fori_loop(0, count, step, 0)

    def columns_of(index):
        return pl.ds(pl.multiple_of(index * S, S), S)

    barrier = pltpu.get_barrier_semaphore()

    def greet(index):
        other = around(me, index, n)
        pl.semaphore_signal(
            barrier, inc=1, device_id=(other,), device_id_type=pl.DeviceIdType.MESH
        )

    each(n - 1, greet)
    fetched = [
        (points_in, points),
        (device_skeleton_in, device_skeleton),
        (charges_in, charges),
        (leaf_basis_in, leaf_basis),
        (device_basis_in, device_basis),
        (group_basis_in, group_own),
        (group_skeleton_in, group_skeleton),
        (cluster_basis_in, cluster_own),
        (cluster_skeleton_in, cluster_skeleton),
        (points_in, window.at[middle_slot, pl.ds(0, F)]),
        (charges_in, window.at[middle_slot, pl.ds(F, R)]),
    ]
    fetches = [
        pltpu.make_async_copy(here, there, local_sem.at[index])
        for index, (here, there) in enumerate(fetched)
    ]
    for index in (0, 1, 9, 10, 2, 3, 4, 5, 6, 7, 8):
        fetches[index].start()

    def lane_offset(index):
        return jnp.where(index < REACH // 2, index - REACH // 2, index - REACH // 2 + 1) * 2

    def lane_copy(index):
        offset = lane_offset(index)
        slot = middle_slot - offset
        return send(
            window.at[middle_slot],
            window.at[slot],
            window_send.at[index],
            window_recv.at[slot],
            jnp.clip(me + offset, 0, n - 1),
        )

    def inside(device):
        return (device >= 0) & (device < n)

    def start_lane(index):
        @pl.when(inside(me + lane_offset(index)))
        def _():
            lane_copy(index).start()

    def forward_copy(index):
        slot = index * 2
        landing = jnp.clip(slot - 1 + 2 * core, 0, 2 * REACH)
        return send(
            window.at[slot],
            window.at[landing],
            forward_send.at[index],
            window_recv.at[landing],
            sibling,
        )

    def forwarded(index):
        slot = index * 2
        landing = slot - 1 + 2 * core
        return inside(me + slot - middle_slot) & (landing >= 0) & (landing <= 2 * REACH)

    def arrived(slot):
        send(
            window.at[slot], window.at[slot], window_send.at[0], window_recv.at[slot], sibling
        ).wait_recv()

    fetches[0].wait()
    fetches[1].wait()
    device_points = jnp.zeros((F, S), jnp.float32)
    for inner in range(LEAVES_DEV):
        rows = slice(inner * leaf, (inner + 1) * leaf)
        device_points += pick(
            points[:, rows], one_hot_of(device_skeleton[...], leaf, inner * leaf)
        )
    device_nodes[child, 0:F, :] = device_points
    for index in range(2, len(fetches)):
        fetches[index].wait()
    pl.semaphore_wait(barrier, n - 1)
    for index in first_sends:
        start_lane(index)
    forward_copy(REACH // 2).start()

    def group_rows_copy(index):
        other = around(child, index, group)
        return send(
            group_own.at[:, columns_of(other)],
            group_rows.at[child],
            rows_send,
            rows_recv,
            group_first + other,
        )

    def cluster_rows_copy(index):
        other = around(place, index, cluster)
        return send(
            cluster_own.at[:, columns_of(other // group)],
            cluster_rows.at[place],
            cluster_rows_send,
            cluster_rows_recv,
            cluster_first + other,
        )

    device_weights = jnp.zeros((R, S), jnp.float32)
    for inner in range(LEAVES_DEV):
        rows = slice(inner * leaf, (inner + 1) * leaf)
        leaf_weights = product(charges[:, rows], leaf_basis[rows, :], 0)
        device_weights += product(
            leaf_weights, device_basis[inner * S : (inner + 1) * S, :], 0
        )
    device_nodes[child, F : F + R, :] = device_weights

    def device_copy(index):
        other = around(child, index, group)
        return send(
            device_nodes.at[child],
            device_nodes.at[child],
            device_send,
            device_recv,
            group_first + other,
        )


    each(group - 1, lambda index: device_copy(index).start())
    for index in second_sends:
        start_lane(index)
    each(group - 1, lambda index: group_rows_copy(index).start())
    each(cluster - 1, lambda index: cluster_rows_copy(index).start())
    group_rows[child] = group_own[:, columns_of(child)]
    cluster_rows[place] = cluster_own[:, columns_of(group_in_cluster)]
    all_of(device_nodes.at[pl.ds(0, group - 1)], device_send, device_recv).wait_recv()

    quarter_weights = jnp.zeros((R, quarter), jnp.float32)
    quarter_points = jnp.zeros((F, quarter), jnp.float32)
    for inner in range(group):
        quarter_weights += product(
            device_nodes[inner, F : F + R, :], group_own[:, inner * S : (inner + 1) * S], 1
        )
        quarter_points += pick(
            device_nodes[inner, 0:F, :], one_hot_of(group_skeleton[...], S, inner * S)
        )
    quarters[place] = jnp.concatenate([quarter_points, quarter_weights], axis=1)

    def quarter_copy(index):
        other = around(place, index, cluster)
        return send(
            quarters.at[place],
            quarters.at[place],
            quarter_send,
            quarter_recv,
            cluster_first + other,
        )


    each(cluster - 1, lambda index: quarter_copy(index).start())
    for index in third_sends:
        start_lane(index)
    all_of(quarters.at[pl.ds(0, cluster - 1)], quarter_send, quarter_recv).wait_recv()

    lane = lax.broadcasted_iota(jnp.int32, (F, 2 * quarter), 1)
    for pair in range(cluster // 2):
        even, odd = quarters[2 * pair], quarters[2 * pair + 1]
        columns = slice(pair * 2 * quarter, (pair + 1) * 2 * quarter)
        stack[0:F, columns] = jnp.where(lane < quarter, even, pltpu.roll(odd, quarter, 1))
        stack[F : F + R, columns] = jnp.where(lane < quarter, pltpu.roll(even, quarter, 1), odd)

    part_points = jnp.zeros((F, part), jnp.float32)
    for inner in range(group):
        part_points += pick(
            stack[0:F, inner * S : (inner + 1) * S],
            one_hot_of(cluster_skeleton[...], S, inner * S),
        )
    part_weights = product(stack[F : F + R, :], cluster_own[...], 1)
    node_rows = jnp.concatenate(
        [part_points, part_weights, jnp.zeros((128 - F - R, part), jnp.float32)], axis=0
    ).T
    parts[me] = node_rows[: part // 2] + pltpu.roll(node_rows[part // 2 :], F + R, 1)

    def part_copy(index):
        return send(
            parts.at[me],
            parts.at[me],
            part_send,
            part_recv,
            around(me, index, n),
        )


    each(n - 1, lambda index: part_copy(index).start())
    for index in fourth_sends:
        start_lane(index)

    group_of = lax.broadcasted_iota(jnp.int32, (R, cluster * quarter), 1) // S
    side_weights = jnp.where(group_of != group_in_cluster, stack[F : F + R, :], 0.0)
    side = far_sum(side_weights, stack[0:F, columns_of(group_in_cluster)], stack[0:F, :])

    def hand_on(index):
        slot = index * 2

        @pl.when(inside(me + slot - middle_slot))
        def _():
            arrived(slot)

            @pl.when(forwarded(index))
            def _():
                forward_copy(index).start()

    for index in early_slots:
        if index != REACH // 2:
            hand_on(index)

    all_of(parts.at[pl.ds(0, n - 1)], part_send, part_recv).wait_recv()
    half = part // 2
    parts_turned[...] = parts[...].reshape(n * half, parts.shape[2]).T
    own_columns = pl.ds(pl.multiple_of((me // cluster) * cluster * half, cluster * half), cluster * half)
    cluster_of = lax.broadcasted_iota(jnp.int32, (R, n * half), 1) // (cluster * half)
    others = cluster_of != me // cluster
    upper = F + R
    all_points = jnp.concatenate(
        [parts_turned[0:F, :], parts_turned[upper : upper + F, :]], axis=1
    )
    all_weights = jnp.concatenate(
        [
            jnp.where(others, parts_turned[F:upper, :], 0.0),
            jnp.where(others, parts_turned[upper + F : upper + F + R, :], 0.0),
        ],
        axis=1,
    )
    own_points = jnp.concatenate(
        [parts_turned[0:F, own_columns], parts_turned[upper : upper + F, own_columns]], axis=1
    )
    top = far_sum(all_weights, own_points, all_points)


    all_of(group_rows.at[pl.ds(0, group - 1)], rows_send, rows_recv).wait_recv()
    all_of(cluster_rows.at[pl.ds(0, cluster - 1)], cluster_rows_send, cluster_rows_recv).wait_recv()

    rows_of_cluster = jnp.concatenate(
        [
            cluster_rows[:, :half, :].reshape(cluster * half, S),
            cluster_rows[:, half:, :].reshape(cluster * half, S),
        ],
        axis=0,
    )
    down_group = side + product(top, rows_of_cluster, 0)
    down_device = product(down_group, group_rows[...].reshape(group * quarter, S), 0)
    for index in late_slots:
        hand_on(index)
    for inner in range(LEAVES_DEV):
        rows = slice(inner * leaf, (inner + 1) * leaf)
        down_leaf = product(down_device, device_basis[inner * S : (inner + 1) * S, :], 1)
        far[:, rows] = product(down_leaf, leaf_basis[rows, :], 1)

    def landed(index):
        slot = index * 2 + 1

        @pl.when(inside(me + slot - middle_slot))
        def _():
            arrived(slot)

    each(REACH, landed)

    def lane_sent(index):
        @pl.when(inside(me + lane_offset(index)))
        def _():
            lane_copy(index).wait_send()

    def forward_sent(index):
        @pl.when(forwarded(index))
        def _():
            forward_copy(index).wait_send()

    each(REACH, lane_sent)
    each(REACH + 1, forward_sent)
    all_of(group_rows.at[pl.ds(0, group - 1)], rows_send, rows_recv).wait_send()
    all_of(cluster_rows.at[pl.ds(0, cluster - 1)], cluster_rows_send, cluster_rows_recv).wait_send()
    all_of(device_nodes.at[pl.ds(0, group - 1)], device_send, device_recv).wait_send()
    all_of(quarters.at[pl.ds(0, cluster - 1)], quarter_send, quarter_recv).wait_send()
    all_of(parts.at[pl.ds(0, n - 1)], part_send, part_recv).wait_send()


def tree(points, charges, leaf_basis, device_basis, device_skeleton, group_basis, group_skeleton,
         cluster_basis, cluster_skeleton):
    n = lax.axis_size("leaf")
    quarter, part = group_basis.shape[1], cluster_basis.shape[1]
    group, cluster = S // quarter, S // part
    width = points.shape[1]
    vmem = pl.BlockSpec(memory_space=pltpu.VMEM)
    dma = pltpu.SemaphoreType.DMA
    return pl.pallas_call(
        functools.partial(tree_kernel, n),
        out_shape=(
            jax.ShapeDtypeStruct((2 * REACH + 1, F + R, width), jnp.float32),
            jax.ShapeDtypeStruct((R, width), jnp.float32),
        ),
        in_specs=[pl.BlockSpec(memory_space=pl.ANY)] * 9,
        out_specs=(pl.BlockSpec(memory_space=pl.ANY), vmem),
        scratch_shapes=[
            pltpu.VMEM(points.shape, jnp.float32),
            pltpu.VMEM(charges.shape, jnp.float32),
            pltpu.VMEM(leaf_basis.shape, jnp.float32),
            pltpu.VMEM(device_basis.shape, jnp.float32),
            pltpu.VMEM(device_skeleton.shape, jnp.int32),
            pltpu.VMEM((quarter, group * S), jnp.float32),
            pltpu.VMEM((1, quarter), jnp.int32),
            pltpu.VMEM((part, group * S), jnp.float32),
            pltpu.VMEM((1, part), jnp.int32),
            pltpu.VMEM((group, quarter, S), jnp.float32),
            pltpu.VMEM((cluster, part, S), jnp.float32),
            pltpu.VMEM((group, F + R, S), jnp.float32),
            pltpu.VMEM((cluster, F, 2 * quarter), jnp.float32),
            pltpu.VMEM((F + R, cluster * quarter), jnp.float32),
            pltpu.VMEM((n, part // 2, 128), jnp.float32),
            pltpu.VMEM((128, n * part // 2), jnp.float32),
            dma((11,)),
            dma((REACH,)),
            dma((REACH + 1,)),
            dma((2 * REACH + 1,)),
            dma(()),
            dma(()),
            dma(()),
            dma(()),
            dma(()),
            dma(()),
            dma(()),
            dma(()),
            dma(()),
            dma(()),
        ],
        compiler_params=pltpu.CompilerParams(
            collective_id=0, has_side_effects=True, vmem_limit_bytes=VMEM_BYTES
        ),
        name="tree_and_window",
    )(
        points,
        charges,
        leaf_basis,
        device_basis,
        device_skeleton,
        group_basis.T,
        group_skeleton[None, :],
        cluster_basis.T,
        cluster_skeleton[None, :],
    )


def shards(points, charges, near_list, near_count, leaf_basis, device_basis, device_skeleton,
           group_basis, group_skeleton, cluster_basis, cluster_skeleton):
    window, far = tree(points, charges, leaf_basis, device_basis, device_skeleton, group_basis,
                       group_skeleton, cluster_basis, cluster_skeleton)
    return near_field(window, near_list, near_count, far)


def solution(mesh):
    return jax.shard_map(
        shards,
        mesh=mesh,
        in_specs=(
            P(None, "leaf"),
            P(None, "leaf"),
            P("leaf", None),
            P("leaf"),
            P("leaf", None),
            P("leaf", None),
            P("leaf", None),
            P(None, "leaf"),
            P("leaf"),
            P(None, "leaf"),
            P("leaf"),
        ),
        out_specs=P(None, "leaf"),
        check_vma=False,
    )
```
